128 devices in a mesh: zg: 4 (over x), ma: 32 (over y, z, core).
Axes of the slice: x: 4, y: 4, z: 4, core: 2. Of those that a mesh axis runs over, the one named last changes fastest.
Arguments:
- forward_coef: bfloat16 [512, 128, 2, 2, 512], P('ma', 'zg'), may hold values from -6 to 6
- adjoint_coef: bfloat16 [512, 128, 2, 2, 512], P('ma', 'zg'), may hold values from -6 to 6
- radial_table: bfloat16 [512, 512, 512], P('ma'), may hold values from -0.25 to 0.25
- radial_count: int32 [512], replicated, may hold values from 1 to 512, as said below
- mode_blocks: int32 [32], replicated, may hold values from 0 to 31, each once
Outputs:
- adjoint_rhs: bfloat16 [512, 128, 2, 2, 512], P('ma', 'zg')
The draws below stay inside these ranges and needn't reach their ends.
Inputs may be any that keep to these rules, and one draw needn't show every extreme that they name: radial_count[m] counts the live radial degrees of azimuthal mode m under a triangular truncation. Each block number appears once; slot block b holds the azimuthal modes mode_blocks[b] * 16 to mode_blocks[b] * 16 + 15.
All inputs are finite; a program needn't handle non-finite values.
Results may differ from the reference program's by a relative error of at most 0.015.
Values may be sent and summed in bfloat16 or wider, within the bound.
A program may use at most 128 MiB of HBM per device.

```python
import math
import jax
import jax.numpy as jnp
from jax import lax

M = 512
NN = 512
NR = 512
K = 128
NPHI = 1024
N_MA = 32


def draw_radial_count(key, part):
    key = jax.random.fold_in(key, 11)
    mode_index = jnp.arange(M, dtype=jnp.int32)
    jitter = jax.random.randint(key, (M,), 0, max(NN // 16, 1) + 1, dtype=jnp.int32)
    jitter = jnp.where(mode_index == 0, 0, jitter)
    base = NN - mode_index * NN // M
    return jnp.maximum(base - jitter, 1).astype(jnp.int32)


def steps_of(key, shape, pieces, low, largest):
    def one(axis_at, parts):
        heights = jax.random.uniform(jax.random.fold_in(jax.random.fold_in(key, 6), axis_at), (parts,), jnp.float32, low / len(pieces), largest / len(pieces))
        return jnp.repeat(jnp.exp(heights), shape[axis_at] // parts).reshape((-1,) + (1,) * (len(shape) - axis_at - 1))

    level = one(*pieces[0])
    for cut in pieces[1:]:
        level = level * one(*cut)
    return level


def bell_draw(key, shape, width, limit, pieces=(), kind=jnp.bfloat16):
    level = steps_of(key, shape, pieces, -0.22, 0.18) if pieces else 1.0
    entries = jax.random.normal(key, shape, jnp.float32) * width * level
    return jnp.minimum(jnp.maximum(entries, -limit), limit).astype(kind)


def setup_inputs(seed: int = 0) -> dict:
    splits = jax.random.split(jax.random.key(seed), 6)
    forward_coef = bell_draw(splits[0], (M, K, 2, 2, NN), 1.0, 6.0, ((0, 32), (1, 4)))
    adjoint_coef = bell_draw(splits[1], (M, K, 2, 2, NN), 1.0, 6.0, ((0, 32), (1, 4)))
    radial_table = bell_draw(splits[2], (M, NN, NR), NN ** -0.5, 0.25, ((0, 32),))
    radial_count = draw_radial_count(jax.random.fold_in(splits[5], 71), 0)
    mode_blocks = jax.random.permutation(splits[4], N_MA).astype(jnp.int32)
    return {"forward_coef": forward_coef, "adjoint_coef": adjoint_coef, "radial_table": radial_table, "radial_count": radial_count, "mode_blocks": mode_blocks}


def rounded(values):
    return lax.optimization_barrier(values.astype(jnp.bfloat16)).astype(jnp.float32)

def build_tables(radial_count, mode_blocks):
    slot_count = M // N_MA
    slot_index = jnp.arange(M, dtype=jnp.int32)
    mode_of_slot = (mode_blocks[slot_index // slot_count] * slot_count + slot_index % slot_count).astype(jnp.int32)
    live_count = radial_count[mode_of_slot]
    live_mask = jnp.arange(NN, dtype=jnp.int32)[None, :] < live_count[:, None]
    point_index = jnp.arange(NPHI, dtype=jnp.int32)
    product_index = mode_of_slot[:, None] * point_index[None, :] % NPHI
    angles = product_index.astype(jnp.float32) * (2.0 * math.pi / NPHI)
    fourier_table = (jnp.stack([jnp.cos(angles), jnp.sin(angles)]) * math.sqrt(2.0 / NPHI)).astype(jnp.bfloat16)
    degree_index = jnp.arange(K, dtype=jnp.int32)
    cheb_index = degree_index[:, None] * (2 * degree_index[None, :] + 1) % (4 * K)
    cheb_angles = cheb_index.astype(jnp.float32) * (math.pi / (2 * K))
    cheb_table = (jnp.cos(cheb_angles) * math.sqrt(2.0 / K)).astype(jnp.bfloat16)
    return (live_mask, fourier_table, cheb_table)

def reference(forward_coef, adjoint_coef, radial_table, radial_count, mode_blocks):
    live_mask, fourier_table, cheb_table = build_tables(radial_count, mode_blocks)
    fourier_wide = fourier_table.astype(jnp.float32)
    cheb_wide = cheb_table.astype(jnp.float32)
    fields = jnp.concatenate([forward_coef, adjoint_coef], axis=3).astype(jnp.float32)
    fields = jnp.where(live_mask[:, None, None, None, :], fields, 0.0)
    block_total = 8
    width_block = NR // block_total
    table_blocks = radial_table.astype(jnp.float32).reshape(M, NN, block_total, width_block).transpose(2, 0, 1, 3)

    def block_step(accumulated, table_block):
        radial_values = rounded(jnp.einsum('mkcfn,mnr->mkcfr', fields, table_block))
        depth_values = rounded(jnp.einsum('mkcfr,kz->zmcfr', radial_values, cheb_wide))
        grid_values = jnp.einsum('zmcfr,cmp->zfrp', depth_values, fourier_wide)
        velocity = grid_values[:, 0]
        heat = grid_values[:, 1]
        velocity_adj = grid_values[:, 2]
        heat_adj = grid_values[:, 3]
        sources = rounded(jnp.stack([velocity * velocity_adj + heat * heat_adj, velocity * heat_adj - heat * velocity_adj], axis=1))
        back_fourier = rounded(jnp.einsum('zgrp,cmp->cmzgr', sources, fourier_wide))
        back_depth = rounded(jnp.einsum('cmzgr,kz->kcmgr', back_fourier, cheb_wide))
        accumulated = accumulated + jnp.einsum('kcmgr,mnr->mkcgn', back_depth, table_block)
        return (accumulated, None)
    start_value = jnp.zeros((M, K, 2, 2, NN), jnp.float32)
    accumulated = lax.scan(block_step, start_value, table_blocks)[0]
    return jnp.where(live_mask[:, None, None, None, :], accumulated, 0.0).astype(jnp.bfloat16)
```

```python
import functools
import math

import jax
import jax.numpy as jnp
import numpy as np
from jax import lax
from jax.experimental import pallas as pl
from jax.experimental.pallas import tpu as pltpu
from jax.sharding import PartitionSpec as P

M = 512
NN = 512
K = 128
NPHI = 1024
MA_DIMS = (4, 4, 2)
MESH = pl.DeviceIdType.MESH
BF16 = jnp.bfloat16
F32 = jnp.float32


def constant_tables():
    index = np.arange(M, dtype=np.int64)[:, None] * np.arange(NPHI, dtype=np.int64)[None, :] % NPHI
    angles = index.astype(np.float64) * (2.0 * math.pi / NPHI)
    fourier = np.concatenate([np.cos(angles), np.sin(angles)]) * math.sqrt(2.0 / NPHI)
    degree = np.arange(K, dtype=np.int64)
    cheb_index = degree[:, None] * (2 * degree[None, :] + 1) % (4 * K)
    cheb = np.cos(cheb_index.astype(np.float64) * (math.pi / (2 * K))) * math.sqrt(2.0 / K)
    fourier = fourier.astype(np.float32).astype(BF16)
    cheb = cheb.astype(np.float32).astype(BF16)
    return fourier, np.ascontiguousarray(fourier.T), cheb, np.ascontiguousarray(cheb.T)


def kernel(dims, rad0, rad1, fourier_hbm, fourier_t_hbm, cheb_ref, cheb_t_ref, mode_row, mode_col, out_ref,
           recv_x, send_y, recv_y, plane, table, table_t, raw, raw_t, grid0, source, send_b, recv_b, send_bx,
           load_sem, local_x, local_y, local_b, local_o, ssem_x, ssem_y, ssem_b, ssem_o, sem_x, sem_y, sem_b, sem_o):
    nx, ma_dims, slots, kd, zd = dims
    ny, nz, nc = ma_dims
    ma = ny * nz * nc
    kk = nx * kd
    x = lax.axis_index("zg")
    m = lax.axis_index("ma")
    my, mz, mc = m // (nz * nc), (m // nc) % nz, m % nc

    def ma_peer(j):
        dy, dz, dc = j // (nz * nc), (j // nc) % nz, j % nc
        return ((my + dy) % ny) * (nz * nc) + ((mz + dz) % nz) * nc + (mc + dc) % nc

    def x_peer(j):
        return (x + j) % nx

    loads = [
        pltpu.make_async_copy(fourier_t_hbm, raw_t, load_sem.at[0]),
        pltpu.make_async_copy(fourier_hbm, raw, load_sem.at[1]),
    ]
    for load in loads:
        load.start()

    barrier = pltpu.get_barrier_semaphore()

    def signal_ma(j, carry):
        pl.semaphore_signal(barrier, inc=1, device_id=(x, ma_peer(j)), device_id_type=MESH)
        return carry

    lax.fori_loop(1, ma, signal_ma, 0)
    for j in range(1, nx):
        pl.semaphore_signal(barrier, inc=1, device_id=(x_peer(j), m), device_id_type=MESH)
    pl.semaphore_wait(barrier, ma - 1 + nx - 1)

    def lane(j):
        return pl.ds(pl.multiple_of(j * 128, 128), 128)

    for ch in range(8):
        field, part = ch // 2, ch % 2
        rad = (rad0, rad1)[field // 2]
        for j in (1, nx - 1) + tuple(range(2, nx - 1)) if nx > 2 else (1,):
            pltpu.make_async_remote_copy(
                src_ref=rad.at[:, part, field % 2, :, lane(x_peer(j))],
                dst_ref=recv_x.at[ch, x],
                send_sem=ssem_x,
                recv_sem=sem_x.at[ch],
                device_id=(x_peer(j), m),
                device_id_type=MESH,
            ).start()
        pltpu.make_async_copy(rad.at[:, part, field % 2, :, lane(x)], recv_x.at[ch, x], local_x.at[ch]).start()

    modes = M
    for load in loads:
        load.wait()
    one_hot = (lax.broadcasted_iota(jnp.int32, (modes, modes), 0) == mode_row[...]).astype(F32).astype(BF16)
    one_hot_t = (lax.broadcasted_iota(jnp.int32, (modes, modes), 1) == mode_col[...]).astype(F32).astype(BF16)
    for part in range(2):
        half = pl.ds(part * modes, modes)
        table_t[:, half] = jnp.dot(raw_t[:, half], one_hot, preferred_element_type=F32).astype(BF16)
        table[half, :] = jnp.dot(one_hot_t, raw[half, :], preferred_element_type=F32).astype(BF16)

    def cheb_chunk(ch, carry):
        pltpu.make_async_copy(recv_x.at[ch, x], recv_x.at[ch, x], local_x.at[ch]).wait()
        pltpu.make_async_remote_copy(
            src_ref=recv_x.at[ch, pl.ds(0, nx - 1)], dst_ref=recv_x.at[ch, pl.ds(0, nx - 1)],
            send_sem=ssem_x, recv_sem=sem_x.at[ch], device_id=(x_peer(1), m), device_id_type=MESH,
        ).wait_recv()
        for s in range(0, slots, 2):
            pair = jnp.concatenate([recv_x[ch, :, s + i].reshape(kk, 128) for i in range(2)], axis=1)
            levels = jnp.dot(cheb_t_ref[...], pair, preferred_element_type=F32)
            for i in range(2):
                plane[pl.ds(s + i, kk, stride=slots), :] = levels[:, 128 * i:128 * (i + 1)]
        send_y[ch] = plane[...].astype(BF16).reshape(ma, zd, slots, 128)

        def send(j, carry):
            peer = ma_peer(j)
            pltpu.make_async_remote_copy(
                src_ref=send_y.at[ch, peer], dst_ref=recv_y.at[ch, m],
                send_sem=ssem_y, recv_sem=sem_y.at[ch], device_id=(x, peer), device_id_type=MESH,
            ).start()
            return carry

        lax.fori_loop(1, ma, send, 0)
        pltpu.make_async_copy(send_y.at[ch, m], recv_y.at[ch, m], local_y.at[ch]).start()
        return carry

    def wait_y(ch, carry):
        pltpu.make_async_copy(recv_y.at[ch, m], recv_y.at[ch, m], local_y.at[ch]).wait()
        pltpu.make_async_remote_copy(
            src_ref=recv_y.at[ch, pl.ds(0, ma - 1)], dst_ref=recv_y.at[ch, pl.ds(0, ma - 1)],
            send_sem=ssem_y, recv_sem=sem_y.at[ch], device_id=(x, ma_peer(1)), device_id_type=MESH,
        ).wait_recv()
        return carry

    def levels_of(arg, z):
        columns = []
        for f2 in range(2):
            first = (arg * 2 + f2) * 2
            columns.append(jnp.concatenate(
                [recv_y[first + part, :, z].reshape(modes, 128) for part in range(2)], axis=0))
        return jnp.concatenate(columns, axis=1)

    lax.fori_loop(0, 5, cheb_chunk, 0)
    lax.fori_loop(0, 4, wait_y, 0)

    def forward_grid(z, carry):
        grid0[z] = jnp.dot(table_t[...], levels_of(0, z), preferred_element_type=F32)
        return carry

    lax.fori_loop(0, zd, forward_grid, 0)
    lax.fori_loop(5, 8, cheb_chunk, 0)
    lax.fori_loop(4, 8, wait_y, 0)

    def back_send(ch, z, count):
        def send(j, carry):
            peer = ma_peer(j)
            pltpu.make_async_remote_copy(
                src_ref=send_b.at[ch, peer, pl.ds(z, count)], dst_ref=recv_b.at[ch, m, pl.ds(z, count)],
                send_sem=ssem_b, recv_sem=sem_b.at[ch], device_id=(x, peer), device_id_type=MESH,
            ).start()
            return carry

        lax.fori_loop(1, ma, send, 0)

    def products(z, carry):
        adjoint = jnp.dot(table_t[...], levels_of(1, z), preferred_element_type=F32)
        velocity, heat = grid0[z, :, :128], grid0[z, :, 128:]
        velocity_adj, heat_adj = adjoint[:, :128], adjoint[:, 128:]
        source[:, :128] = (velocity * velocity_adj + heat * heat_adj).astype(BF16)
        source[:, 128:] = (velocity * heat_adj - heat * velocity_adj).astype(BF16)
        back = jnp.dot(table[...], source[...], preferred_element_type=F32).astype(BF16)
        for g in range(2):
            for part in range(2):
                send_b[g * 2 + part, :, z] = back[part * modes:(part + 1) * modes,
                                                  128 * g:128 * (g + 1)].reshape(ma, slots, 128)
        back_send(0, z, 1)
        return carry

    lax.fori_loop(0, zd, products, 0)
    for ch in range(1, 4):
        back_send(ch, 0, zd)
    for ch in range(4):
        pltpu.make_async_copy(send_b.at[ch, m], recv_b.at[ch, m], local_b.at[ch]).start()

    for ch in range(4):
        g, part = ch // 2, ch % 2
        pltpu.make_async_copy(recv_b.at[ch, m], recv_b.at[ch, m], local_b.at[ch]).wait()
        pltpu.make_async_remote_copy(
            src_ref=recv_b.at[ch, pl.ds(0, ma - 1)], dst_ref=recv_b.at[ch, pl.ds(0, ma - 1)],
            send_sem=ssem_b, recv_sem=sem_b.at[ch], device_id=(x, ma_peer(1)), device_id_type=MESH,
        ).wait_recv()
        plane[...] = recv_b[ch].reshape(kk * slots, 128).astype(F32)
        for s in range(0, slots, 2):
            pair = jnp.concatenate([plane[pl.ds(s + i, kk, stride=slots), :] for i in range(2)], axis=1).astype(BF16)
            degrees = jnp.dot(cheb_ref[...], pair, preferred_element_type=F32).astype(BF16)
            for i in range(2):
                send_bx[ch, :, s + i] = degrees[:, 128 * i:128 * (i + 1)].reshape(nx, kd, 128)
        for j in (1, nx - 1) + tuple(range(2, nx - 1)) if nx > 2 else (1,):
            pltpu.make_async_remote_copy(
                src_ref=send_bx.at[ch, x_peer(j)], dst_ref=out_ref.at[:, part, g, :, lane(x)],
                send_sem=ssem_o, recv_sem=sem_o.at[ch], device_id=(x_peer(j), m), device_id_type=MESH,
            ).start()
        pltpu.make_async_copy(send_bx.at[ch, x], out_ref.at[:, part, g, :, lane(x)], local_o.at[ch]).start()

    for ch in range(4):
        g, part = ch // 2, ch % 2
        pltpu.make_async_copy(send_bx.at[ch, x], out_ref.at[:, part, g, :, lane(x)], local_o.at[ch]).wait()
        pltpu.make_async_remote_copy(
            src_ref=send_bx.at[ch, pl.ds(0, nx - 1)], dst_ref=send_bx.at[ch, pl.ds(0, nx - 1)],
            send_sem=ssem_o, recv_sem=sem_o.at[ch], device_id=(x_peer(1), m), device_id_type=MESH,
        ).wait()
    for buffer, count, sem in ((recv_x, nx - 1, ssem_x), (recv_y, ma - 1, ssem_y), (recv_b, ma - 1, ssem_b)):
        part_ref = buffer.at[:, pl.ds(0, count)]
        pltpu.make_async_remote_copy(
            src_ref=part_ref, dst_ref=part_ref, send_sem=sem, recv_sem=sem,
            device_id=(x_peer(1), m), device_id_type=MESH,
        ).wait_send()


def middle(ma_dims, rad0, rad1, mode_of_slot):
    nx = lax.axis_size("zg")
    ma = lax.axis_size("ma")
    slots, _, _, kd, _ = rad0.shape
    kk = nx * kd
    zd = kk // ma
    fourier, fourier_t, cheb, cheb_t = constant_tables()
    any_spec = pl.BlockSpec(memory_space=pl.ANY)
    vmem_spec = pl.BlockSpec(memory_space=pltpu.VMEM)
    dma = pltpu.SemaphoreType.DMA
    return pl.pallas_call(
        functools.partial(kernel, (nx, ma_dims, slots, kd, zd)),
        out_shape=jax.ShapeDtypeStruct((slots, 2, 2, kd, nx * 128), BF16),
        in_specs=[any_spec] * 4 + [vmem_spec] * 4,
        out_specs=any_spec,
        scratch_shapes=[
            pltpu.VMEM((8, nx, slots, kd, 128), BF16),
            pltpu.VMEM((8, ma, zd, slots, 128), BF16),
            pltpu.VMEM((8, ma, zd, slots, 128), BF16),
            pltpu.VMEM((kk * slots, 128), F32),
            pltpu.VMEM((2 * M, NPHI), BF16),
            pltpu.VMEM((NPHI, 2 * M), BF16),
            pltpu.VMEM((2 * M, NPHI), BF16),
            pltpu.VMEM((NPHI, 2 * M), BF16),
            pltpu.VMEM((zd, NPHI, 256), F32),
            pltpu.VMEM((NPHI, 256), BF16),
            pltpu.VMEM((4, ma, zd, slots, 128), BF16),
            pltpu.VMEM((4, ma, zd, slots, 128), BF16),
            pltpu.VMEM((4, nx, slots, kd, 128), BF16),
            dma((2,)), dma((8,)), dma((8,)), dma((4,)), dma((4,)),
            dma, dma, dma, dma,
            dma((8,)), dma((8,)), dma((4,)), dma((4,)),
        ],
        compiler_params=pltpu.CompilerParams(
            collective_id=1, has_side_effects=True, vmem_limit_bytes=56 * 2**20
        ),
    )(rad0, rad1, jnp.asarray(fourier), jnp.asarray(fourier_t), jnp.asarray(cheb), jnp.asarray(cheb_t),
      mode_of_slot.reshape(1, M), mode_of_slot.reshape(M, 1))


def body(ma_dims, forward_coef, adjoint_coef, radial_table, radial_count, mode_blocks):
    slots = forward_coef.shape[0]
    group = jnp.arange(lax.axis_size("ma"), dtype=jnp.int32)
    own_block = jnp.sum(jnp.where(group == lax.axis_index("ma"), mode_blocks, 0))
    slot_index = jnp.arange(slots, dtype=jnp.int32)
    own_modes = own_block * slots + slot_index
    mode_of_slot = (mode_blocks[:, None] * slots + slot_index[None, :]).reshape(M)
    mode_index = jnp.arange(M, dtype=jnp.int32)
    live_count = jnp.sum(jnp.where(own_modes[:, None] == mode_index[None, :], radial_count[None, :], 0), axis=1)
    live = jnp.arange(NN, dtype=jnp.int32)[None, :] < live_count[:, None]
    masked_table = jnp.where(live[:, :, None], radial_table, jnp.zeros((), BF16))
    radial = [
        jnp.einsum("skcfn,snr->scfkr", coef, masked_table, preferred_element_type=F32).astype(BF16)
        for coef in (forward_coef, adjoint_coef)
    ]
    back = middle(ma_dims, radial[0], radial[1], mode_of_slot)
    return jnp.einsum("scgkr,snr->skcgn", back, masked_table, preferred_element_type=F32).astype(BF16)


def solution(mesh):
    placed = (P("ma", "zg", None, None, None), P("ma", "zg", None, None, None), P("ma", None, None), P(), P())
    return jax.shard_map(
        functools.partial(body, MA_DIMS), mesh=mesh, in_specs=placed,
        out_specs=P("ma", "zg", None, None, None), check_vma=False,
    )
```

```python
import functools
import math

import jax
import jax.numpy as jnp
import numpy as np
from jax import lax
from jax.experimental import pallas as pl
from jax.experimental.pallas import tpu as pltpu
from jax.sharding import PartitionSpec as P

M = 512
NN = 512
K = 128
NPHI = 1024
MA_DIMS = (4, 4, 2)
MESH = pl.DeviceIdType.MESH
BF16 = jnp.bfloat16
F32 = jnp.float32


def constant_tables():
    index = np.arange(M, dtype=np.int64)[:, None] * np.arange(NPHI, dtype=np.int64)[None, :] % NPHI
    angles = index.astype(np.float64) * (2.0 * math.pi / NPHI)
    fourier = np.concatenate([np.cos(angles), np.sin(angles)]) * math.sqrt(2.0 / NPHI)
    degree = np.arange(K, dtype=np.int64)
    cheb_index = degree[:, None] * (2 * degree[None, :] + 1) % (4 * K)
    cheb = np.cos(cheb_index.astype(np.float64) * (math.pi / (2 * K))) * math.sqrt(2.0 / K)
    fourier = fourier.astype(np.float32).astype(BF16)
    cheb = cheb.astype(np.float32).astype(BF16)
    return fourier, np.ascontiguousarray(fourier.T), cheb, np.ascontiguousarray(cheb.T)


def kernel(dims, coef0, coef1, radial_hbm, fourier_hbm, fourier_t_hbm, cheb_ref, cheb_t_ref, count_ref, block_ref,
           out_ref, coef, radial, wide, send_x, recv_x, send_y, recv_y, plane, one_hot, raw, raw_t, table, table_t,
           source, send_b, recv_b, send_o, recv_o, wide_out, out_v,
           coef_sem, radial_sem, load_sem, out_sem, local_x, local_y, local_b, local_o,
           ssem_x, ssem_y, ssem_b, ssem_o, sem_x, sem_y, sem_b, sem_o):
    nx, ma_dims, slots, kd, zd, nbs = dims
    ny, nz, nc = ma_dims
    ma = ny * nz * nc
    kk = nx * kd
    modes = ma * slots
    row_step = 4 * nbs
    x = lax.axis_index("zg")
    m = lax.axis_index("ma")
    my, mz, mc = m // (nz * nc), (m // nc) % nz, m % nc
    x_order = (1,) if nx == 2 else (1, nx - 1) + tuple(range(2, nx - 1))

    def ma_peer(j):
        dy, dz, dc = j // (nz * nc), (j // nc) % nz, j % nc
        return ((my + dy) % ny) * (nz * nc) + ((mz + dz) % nz) * nc + (mc + dc) % nc

    def x_peer(j):
        return (x + j) % nx

    def remote(src, dst, send_sem, recv_sem, to_x, to_m):
        return pltpu.make_async_remote_copy(
            src_ref=src, dst_ref=dst, send_sem=send_sem, recv_sem=recv_sem,
            device_id=(to_x, to_m), device_id_type=MESH,
        )

    def wait_received(buffer, ch, count, sem, local_sem):
        own = buffer.at[ch, 0]
        pltpu.make_async_copy(own, own, local_sem.at[ch]).wait()
        others = buffer.at[ch, pl.ds(0, count)]
        remote(others, others, sem.at[ch], sem.at[ch], x_peer(1), m).wait_recv()

    barrier = pltpu.get_barrier_semaphore()

    def signal_ma(j, carry):
        pl.semaphore_signal(barrier, inc=1, device_id=(x, ma_peer(j)), device_id_type=MESH)
        return carry

    lax.fori_loop(1, ma, signal_ma, 0)
    for j in range(1, nx):
        pl.semaphore_signal(barrier, inc=1, device_id=(x_peer(j), m), device_id_type=MESH)

    def coef_load(arg, s):
        return pltpu.make_async_copy((coef0, coef1)[arg].at[s], coef.at[arg, s], coef_sem.at[arg, s])

    def radial_load(s):
        return pltpu.make_async_copy(radial_hbm.at[s], radial.at[s], radial_sem.at[s])

    def start_first(s, carry):
        coef_load(0, s).start()
        radial_load(s).start()
        return carry

    def start_second(s, carry):
        coef_load(1, s).start()
        return carry

    lax.fori_loop(0, slots, start_first, 0)
    lax.fori_loop(0, slots, start_second, 0)
    loads = [
        pltpu.make_async_copy(fourier_t_hbm, raw_t, load_sem.at[0]),
        pltpu.make_async_copy(fourier_hbm, raw, load_sem.at[1]),
    ]
    for load in loads:
        load.start()

    own_block = block_ref[m]
    lanes = lax.broadcasted_iota(jnp.int32, (1, 128), 1)
    low = lanes < 64

    def radial_slot(arg, s):
        coef_load(arg, s).wait()
        if arg == 0:
            radial_load(s).wait()
        live = count_ref[own_block * slots + s]
        wide[...] = coef[arg, s].astype(F32)
        rows = []
        for f in range(2):
            for part in range(2):
                tiles = []
                for nb in range(nbs):
                    tile = wide[pl.ds((part * nbs + nb) * 2 + f, kd, stride=row_step), :]
                    tiles.append(jnp.where(lanes + nb * 128 < live, tile, 0.0).astype(BF16))
                rows.append(jnp.concatenate(tiles, axis=1))
        values = jnp.dot(jnp.concatenate(rows, axis=0), radial[s], preferred_element_type=F32)
        for to in range(nx):
            first = values[:2 * kd, 128 * to:128 * (to + 1)]
            second = pltpu.roll(values[2 * kd:, 128 * to:128 * (to + 1)], 64, 1)
            halves = (jnp.where(low, first, second).astype(BF16), jnp.where(low, second, first).astype(BF16))
            for h in range(2):
                for part in range(2):
                    send_x[h * 4 + arg * 2 + part, to, s] = halves[h][part * kd:(part + 1) * kd]

    def x_send(ch):
        for j in x_order:
            remote(send_x.at[ch, x_peer(j)], recv_x.at[ch, x], ssem_x, sem_x.at[ch], x_peer(j), m).start()
        pltpu.make_async_copy(send_x.at[ch, x], recv_x.at[ch, x], local_x.at[ch]).start()

    def radial_first(s, carry):
        radial_slot(0, s)
        return carry

    def radial_second(s, carry):
        radial_slot(1, s)
        return carry

    lax.fori_loop(0, slots, radial_first, 0)
    pl.semaphore_wait(barrier, ma - 1 + nx - 1)
    for ch in (0, 1):
        x_send(ch)
    lax.fori_loop(0, slots, radial_second, 0)
    for ch in (2, 3, 4, 5, 6, 7):
        x_send(ch)

    def one_hot_block(j, carry):
        start = pl.multiple_of(j * slots, slots)
        column = lax.broadcasted_iota(jnp.int32, (slots, modes), 1)
        row = lax.broadcasted_iota(jnp.int32, (slots, modes), 0)
        one_hot[pl.ds(start, slots), :] = (column == row + block_ref[j] * slots).astype(F32).astype(BF16)
        return carry

    lax.fori_loop(0, ma, one_hot_block, 0)
    for load in loads:
        load.wait()
    for part in range(2):
        half = pl.ds(part * modes, modes)
        table_t[:, half] = lax.dot_general(
            raw_t[:, half], one_hot[...], (((1,), (1,)), ((), ())), preferred_element_type=F32).astype(BF16)
        table[half, :] = jnp.dot(one_hot[...], raw[half, :], preferred_element_type=F32).astype(BF16)

    def cheb_chunk(ch, carry):
        wait_received(recv_x, ch, nx - 1, sem_x, local_x)
        for s in range(0, slots, 2):
            pair = jnp.concatenate([recv_x[ch, :, s + i].reshape(kk, 128) for i in range(2)], axis=1)
            levels = jnp.dot(cheb_t_ref[...], pair, preferred_element_type=F32)
            for i in range(2):
                plane[pl.ds(s + i, kk, stride=slots), :] = levels[:, 128 * i:128 * (i + 1)]
        send_y[ch] = plane[...].astype(BF16).reshape(ma, zd, slots, 128)

        def send(j, carry):
            peer = ma_peer(j)
            remote(send_y.at[ch, peer], recv_y.at[ch, m], ssem_y, sem_y.at[ch], x, peer).start()
            return carry

        lax.fori_loop(1, ma, send, 0)
        pltpu.make_async_copy(send_y.at[ch, m], recv_y.at[ch, m], local_y.at[ch]).start()
        return carry

    def wait_y(ch, carry):
        wait_received(recv_y, ch, ma - 1, sem_y, local_y)
        return carry

    def products(h, z):
        columns = []
        for i in range(2):
            for arg in range(2):
                columns.append(jnp.concatenate(
                    [recv_y[h * 4 + arg * 2 + part, :, z + i].reshape(modes, 128) for part in range(2)], axis=0))
        grid = jnp.dot(table_t[...], jnp.concatenate(columns, axis=1), preferred_element_type=F32)
        for i in range(2):
            forward = grid[:, 256 * i:256 * i + 128]
            adjoint = grid[:, 256 * i + 128:256 * i + 256]
            straight = forward * adjoint
            crossed = forward * pltpu.roll(adjoint, 64, 1)
            first = straight + pltpu.roll(straight, 64, 1)
            second = pltpu.roll(crossed, 64, 1) - crossed
            pick = (first, second) if h == 0 else (second, first)
            source[:, 128 * i:128 * (i + 1)] = jnp.where(low, pick[0], pick[1]).astype(BF16)
        back = jnp.dot(table[...], source[...], preferred_element_type=F32).astype(BF16)
        for i in range(2):
            for part in range(2):
                send_b[h * 2 + part, :, z + i] = back[part * modes:(part + 1) * modes,
                                                      128 * i:128 * (i + 1)].reshape(ma, slots, 128)

    def back_send(ch):
        def send(j, carry):
            peer = ma_peer(j)
            remote(send_b.at[ch, peer], recv_b.at[ch, m], ssem_b, sem_b.at[ch], x, peer).start()
            return carry

        lax.fori_loop(1, ma, send, 0)
        pltpu.make_async_copy(send_b.at[ch, m], recv_b.at[ch, m], local_b.at[ch]).start()

    lax.fori_loop(0, 5, cheb_chunk, 0)
    lax.fori_loop(0, 4, wait_y, 0)
    for step in range(zd // 2):
        products(0, 2 * step)
        if step == 0:
            lax.fori_loop(5, 6, cheb_chunk, 0)
    lax.fori_loop(6, 8, cheb_chunk, 0)
    for ch in (0, 1):
        back_send(ch)
    lax.fori_loop(4, 8, wait_y, 0)
    for step in range(zd // 2):
        products(1, 2 * step)
    for ch in (2, 3):
        back_send(ch)

    def cheb_back(ch, carry):
        wait_received(recv_b, ch, ma - 1, sem_b, local_b)
        plane[...] = recv_b[ch].reshape(kk * slots, 128).astype(F32)
        for s in range(0, slots, 2):
            pair = jnp.concatenate([plane[pl.ds(s + i, kk, stride=slots), :] for i in range(2)], axis=1).astype(BF16)
            degrees = jnp.dot(cheb_ref[...], pair, preferred_element_type=F32).astype(BF16)
            for i in range(2):
                send_o[ch, :, s + i] = degrees[:, 128 * i:128 * (i + 1)].reshape(nx, kd, 128)
        for j in x_order:
            remote(send_o.at[ch, x_peer(j)], recv_o.at[ch, x], ssem_o, sem_o.at[ch], x_peer(j), m).start()
        pltpu.make_async_copy(send_o.at[ch, x], recv_o.at[ch, x], local_o.at[ch]).start()
        return carry

    lax.fori_loop(0, 4, cheb_back, 0)

    def out_copy(s):
        return pltpu.make_async_copy(out_v.at[s], out_ref.at[s], out_sem.at[s])

    def radial_back(part, s):
        live = count_ref[own_block * slots + s]
        first, second = [], []
        for at in range(nx):
            near = recv_o[part, at, s].astype(F32)
            far = recv_o[2 + part, at, s].astype(F32)
            first.append(jnp.where(low, near, far).astype(BF16))
            second.append(pltpu.roll(jnp.where(low, far, near), 64, 1).astype(BF16))
        rows = jnp.concatenate([jnp.concatenate(first, axis=1), jnp.concatenate(second, axis=1)], axis=0)
        values = lax.dot_general(rows, radial[s], (((1,), (1,)), ((), ())), preferred_element_type=F32)
        for g in range(2):
            for nb in range(nbs):
                tile = values[g * kd:(g + 1) * kd, 128 * nb:128 * (nb + 1)]
                wide_out[s, pl.ds((part * nbs + nb) * 2 + g, kd, stride=row_step), :] = jnp.where(
                    lanes + nb * 128 < live, tile, 0.0)
        if part == 1:
            out_v[s] = wide_out[s].astype(BF16)
            out_copy(s).start()

    def radial_back_first(s, carry):
        radial_back(0, s)
        return carry

    def radial_back_second(s, carry):
        radial_back(1, s)
        return carry

    for ch in (0, 2):
        wait_received(recv_o, ch, nx - 1, sem_o, local_o)
    lax.fori_loop(0, slots, radial_back_first, 0)
    for ch in (1, 3):
        wait_received(recv_o, ch, nx - 1, sem_o, local_o)
    lax.fori_loop(0, slots, radial_back_second, 0)

    def finish(s, carry):
        out_copy(s).wait()
        return carry

    lax.fori_loop(0, slots, finish, 0)
    for buffer, count, sem in (
        (recv_x, nx - 1, ssem_x), (recv_y, ma - 1, ssem_y), (recv_b, ma - 1, ssem_b), (recv_o, nx - 1, ssem_o)
    ):
        sent = buffer.at[:, pl.ds(0, count)]
        remote(sent, sent, sem, sem, x_peer(1), m).wait_send()


def body(ma_dims, forward_coef, adjoint_coef, radial_table, radial_count, mode_blocks):
    nx = lax.axis_size("zg")
    ma = lax.axis_size("ma")
    slots, kd = forward_coef.shape[:2]
    kk = nx * kd
    zd = kk // ma
    nbs = NN // 128
    coef_rows = kd * 2 * nbs * 2

    def to_rows(array):
        blocks = array.reshape(slots, kd * 2, 2, nbs, 128).transpose(0, 1, 3, 2, 4)
        return blocks.reshape(slots, coef_rows, 128)

    fourier, fourier_t, cheb, cheb_t = constant_tables()
    any_spec = pl.BlockSpec(memory_space=pl.ANY)
    vmem_spec = pl.BlockSpec(memory_space=pltpu.VMEM)
    smem_spec = pl.BlockSpec(memory_space=pltpu.SMEM)
    dma = pltpu.SemaphoreType.DMA
    rows = pl.pallas_call(
        functools.partial(kernel, (nx, ma_dims, slots, kd, zd, nbs)),
        out_shape=jax.ShapeDtypeStruct((slots, coef_rows, 128), BF16),
        in_specs=[any_spec] * 5 + [vmem_spec] * 2 + [smem_spec] * 2,
        out_specs=any_spec,
        scratch_shapes=[
            pltpu.VMEM((2, slots, coef_rows, 128), BF16),
            pltpu.VMEM(radial_table.shape, BF16),
            pltpu.VMEM((coef_rows, 128), F32),
            pltpu.VMEM((8, nx, slots, kd, 128), BF16),
            pltpu.VMEM((8, nx, slots, kd, 128), BF16),
            pltpu.VMEM((8, ma, zd, slots, 128), BF16),
            pltpu.VMEM((8, ma, zd, slots, 128), BF16),
            pltpu.VMEM((kk * slots, 128), F32),
            pltpu.VMEM((M, M), BF16),
            pltpu.VMEM((2 * M, NPHI), BF16),
            pltpu.VMEM((NPHI, 2 * M), BF16),
            pltpu.VMEM((2 * M, NPHI), BF16),
            pltpu.VMEM((NPHI, 2 * M), BF16),
            pltpu.VMEM((NPHI, 256), BF16),
            pltpu.VMEM((4, ma, zd, slots, 128), BF16),
            pltpu.VMEM((4, ma, zd, slots, 128), BF16),
            pltpu.VMEM((4, nx, slots, kd, 128), BF16),
            pltpu.VMEM((4, nx, slots, kd, 128), BF16),
            pltpu.VMEM((slots, coef_rows, 128), F32),
            pltpu.VMEM((slots, coef_rows, 128), BF16),
            dma((2, slots)), dma((slots,)), dma((2,)), dma((slots,)),
            dma((8,)), dma((8,)), dma((4,)), dma((4,)),
            dma, dma, dma, dma,
            dma((8,)), dma((8,)), dma((4,)), dma((4,)),
        ],
        compiler_params=pltpu.CompilerParams(
            collective_id=1, has_side_effects=True, vmem_limit_bytes=60 * 2**20
        ),
    )(to_rows(forward_coef), to_rows(adjoint_coef), radial_table, jnp.asarray(fourier), jnp.asarray(fourier_t),
      jnp.asarray(cheb), jnp.asarray(cheb_t), radial_count, mode_blocks)
    blocks = rows.reshape(slots, kd * 2, nbs, 2, 128).transpose(0, 1, 3, 2, 4)
    return blocks.reshape(forward_coef.shape)


def solution(mesh):
    placed = (P("ma", "zg", None, None, None), P("ma", "zg", None, None, None), P("ma", None, None), P(), P())
    return jax.shard_map(
        functools.partial(body, MA_DIMS), mesh=mesh, in_specs=placed,
        out_specs=P("ma", "zg", None, None, None), check_vma=False,
    )
```

```python
import functools
import math

import jax
import jax.numpy as jnp
import numpy as np
from jax import lax
from jax.experimental import pallas as pl
from jax.experimental.pallas import tpu as pltpu
from jax.sharding import PartitionSpec as P

M = 512
NN = 512
K = 128
NPHI = 1024
MA_DIMS = (4, 4, 2)
MESH = pl.DeviceIdType.MESH
BF16 = jnp.bfloat16
F32 = jnp.float32


def constant_tables():
    index = np.arange(M, dtype=np.int64)[:, None] * np.arange(NPHI, dtype=np.int64)[None, :] % NPHI
    angles = index.astype(np.float64) * (2.0 * math.pi / NPHI)
    fourier = np.concatenate([np.cos(angles), np.sin(angles)]) * math.sqrt(2.0 / NPHI)
    degree = np.arange(K, dtype=np.int64)
    cheb_index = degree[:, None] * (2 * degree[None, :] + 1) % (4 * K)
    cheb = np.cos(cheb_index.astype(np.float64) * (math.pi / (2 * K))) * math.sqrt(2.0 / K)
    fourier = fourier.astype(np.float32).astype(BF16)
    cheb = cheb.astype(np.float32).astype(BF16)
    return fourier, np.ascontiguousarray(fourier.T), cheb, np.ascontiguousarray(cheb.T)


def kernel(dims, coef0, coef1, radial_hbm, fourier_hbm, fourier_t_hbm, cheb_ref, cheb_t_ref, count_ref, block_ref,
           out_ref, coef, radial, wide, send_x, recv_x, send_y, recv_y, plane, one_hot, raw, raw_t, table, table_t,
           source, send_b, recv_b, send_o, recv_o,
           coef_sem, radial_sem, load_sem, local_x, local_y, local_b, local_o,
           ssem_x, ssem_y, ssem_b, ssem_o, sem_x, sem_y, sem_b, sem_o):
    nx, ma_dims, slots, kd, zd, nbs = dims
    ny, nz, nc = ma_dims
    ma = ny * nz * nc
    kk = nx * kd
    modes = ma * slots
    row_step = 4 * nbs
    x = lax.axis_index("zg")
    m = lax.axis_index("ma")
    my, mz, mc = m // (nz * nc), (m // nc) % nz, m % nc
    half = slots // 2
    x_order = (1,) if nx == 2 else tuple(range(2, nx - 1)) + (1, nx - 1)

    def far_first(i, n):
        return (2 + i + (i // 2) * (1 + 2 * (i % 2))) % 4 if n == 4 else n - 1 - i

    def ma_peer(j):
        dy, dz, dc = far_first(j // (nz * nc), ny), far_first((j // nc) % nz, nz), nc - 1 - j % nc
        return ((my + dy) % ny) * (nz * nc) + ((mz + dz) % nz) * nc + (mc + dc) % nc

    def x_peer(j):
        return (x + j) % nx

    def remote(src, dst, send_sem, recv_sem, to_x, to_m):
        return pltpu.make_async_remote_copy(
            src_ref=src, dst_ref=dst, send_sem=send_sem, recv_sem=recv_sem,
            device_id=(to_x, to_m), device_id_type=MESH,
        )

    def wait_received(buffer, ch, count, sem, local_sem):
        own = buffer.at[ch, 0]
        pltpu.make_async_copy(own, own, local_sem.at[ch]).wait()
        others = buffer.at[ch, pl.ds(0, count)]
        remote(others, others, sem.at[ch], sem.at[ch], x_peer(1), m).wait_recv()

    barrier = pltpu.get_barrier_semaphore()

    def signal_ma(j, carry):
        pl.semaphore_signal(barrier, inc=1, device_id=(x, ma_peer(j)), device_id_type=MESH)
        return carry

    lax.fori_loop(0, ma - 1, signal_ma, 0)
    for j in range(1, nx):
        pl.semaphore_signal(barrier, inc=1, device_id=(x_peer(j), m), device_id_type=MESH)

    def coef_load(arg, s):
        return pltpu.make_async_copy((coef0, coef1)[arg].at[s], coef.at[arg, s], coef_sem.at[arg, s])

    def radial_load(s):
        return pltpu.make_async_copy(radial_hbm.at[s], radial.at[s], radial_sem.at[s])

    def start_first(s, carry):
        coef_load(0, s).start()
        radial_load(s).start()
        return carry

    def start_second(s, carry):
        coef_load(1, s).start()
        return carry

    lax.fori_loop(0, slots, start_first, 0)
    lax.fori_loop(0, slots, start_second, 0)
    loads = [
        pltpu.make_async_copy(fourier_t_hbm, raw_t, load_sem.at[0]),
        pltpu.make_async_copy(fourier_hbm, raw, load_sem.at[1]),
    ]
    for load in loads:
        load.start()

    own_block = block_ref[m]
    lanes = lax.broadcasted_iota(jnp.int32, (1, 128), 1)
    low = lanes < 64

    def radial_slot(arg, s):
        coef_load(arg, s).wait()
        if arg == 0:
            radial_load(s).wait()
        live = count_ref[own_block * slots + s]
        wide[...] = coef[arg, s].astype(F32)
        rows = []
        for f in range(2):
            for part in range(2):
                tiles = []
                for nb in range(nbs):
                    tile = wide[pl.ds((part * nbs + nb) * 2 + f, kd, stride=row_step), :]
                    tiles.append(jnp.where(lanes + nb * 128 < live, tile, 0.0).astype(BF16))
                rows.append(jnp.concatenate(tiles, axis=1))
        values = jnp.dot(jnp.concatenate(rows, axis=0), radial[s], preferred_element_type=F32)
        for to in range(nx):
            first = values[:2 * kd, 128 * to:128 * (to + 1)]
            second = pltpu.roll(values[2 * kd:, 128 * to:128 * (to + 1)], 64, 1)
            halves = (jnp.where(low, first, second).astype(BF16), jnp.where(low, second, first).astype(BF16))
            for h in range(2):
                for part in range(2):
                    ch = ((h * 2 + arg) * 2 + s // half) * 2 + part
                    send_x[ch, to, s % half] = halves[h][part * kd:(part + 1) * kd]

    def x_send(ch):
        for j in x_order:
            remote(send_x.at[ch, x_peer(j)], recv_x.at[ch, x], ssem_x, sem_x.at[ch], x_peer(j), m).start()
        pltpu.make_async_copy(send_x.at[ch, x], recv_x.at[ch, x], local_x.at[ch]).start()

    def radial_first(s, carry):
        radial_slot(0, s)
        return carry

    def radial_second(s, carry):
        radial_slot(1, s)
        return carry

    lax.fori_loop(0, slots, radial_first, 0)
    pl.semaphore_wait(barrier, ma - 1 + nx - 1)
    for ch in range(4):
        x_send(ch)
    lax.fori_loop(0, slots, radial_second, 0)

    def one_hot_block(i, carry):
        part, pair = i // (ma // 2), i % (ma // 2)
        start = pl.multiple_of(i * 2 * half, 2 * half)
        column = lax.broadcasted_iota(jnp.int32, (2 * half, modes), 1)
        row = lax.broadcasted_iota(jnp.int32, (2 * half, modes), 0)
        first, second = block_ref[2 * pair] * slots, block_ref[2 * pair + 1] * slots
        mode = jnp.where(row < half, first + row, second + row - half) + part * half
        one_hot[pl.ds(start, 2 * half), :] = (column == mode).astype(F32).astype(BF16)
        return carry

    def make_tables():
        lax.fori_loop(0, ma, one_hot_block, 0)
        for load in loads:
            load.wait()
        for part in range(2):
            span = pl.ds(part * modes, modes)
            table_t[:, span] = lax.dot_general(
                raw_t[:, span], one_hot[...], (((1,), (1,)), ((), ())), preferred_element_type=F32).astype(BF16)
            table[span, :] = jnp.dot(one_hot[...], raw[span, :], preferred_element_type=F32).astype(BF16)

    def cheb_chunk(ahead, ch, carry):
        wait_received(recv_x, ch, nx - 1, sem_x, local_x)
        if ahead:
            x_send(ch + ahead)
        for s in range(0, half, 2):
            pair = jnp.concatenate([recv_x[ch, :, s + i].reshape(kk, 128) for i in range(2)], axis=1)
            levels = jnp.dot(cheb_t_ref[...], pair, preferred_element_type=F32)
            for i in range(2):
                plane[pl.ds(s + i, kk, stride=half), :] = levels[:, 128 * i:128 * (i + 1)]
        send_y[ch] = plane[...].astype(BF16).reshape(ma, zd // 2, 2 * half, 128)

        def send(j, carry):
            peer = ma_peer(j)
            remote(send_y.at[ch, peer], recv_y.at[ch, m], ssem_y, sem_y.at[ch], x, peer).start()
            return carry

        lax.fori_loop(0, ma - 1, send, 0)
        pltpu.make_async_copy(send_y.at[ch, m], recv_y.at[ch, m], local_y.at[ch]).start()
        return carry

    def wait_y(ch, carry):
        wait_received(recv_y, ch, ma - 1, sem_y, local_y)
        return carry

    def products(h, pair):
        columns = []
        for arg in range(2):
            levels = [[], []]
            for part in range(2):
                for sh in range(2):
                    tiles = recv_y[((h * 2 + arg) * 2 + sh) * 2 + part, :, pair].astype(F32)
                    tiles = tiles.reshape(ma, 2, half, 128)
                    for i in range(2):
                        levels[i].append(tiles[:, i].reshape(ma * half, 128).astype(BF16))
            columns.append([jnp.concatenate(level, axis=0) for level in levels])
        columns = [columns[arg][i] for i in range(2) for arg in range(2)]
        grid = jnp.dot(table_t[...], jnp.concatenate(columns, axis=1), preferred_element_type=F32)
        for i in range(2):
            forward = grid[:, 256 * i:256 * i + 128]
            adjoint = grid[:, 256 * i + 128:256 * i + 256]
            straight = forward * adjoint
            crossed = forward * pltpu.roll(adjoint, 64, 1)
            first = straight + pltpu.roll(straight, 64, 1)
            second = pltpu.roll(crossed, 64, 1) - crossed
            pick = (first, second) if h == 0 else (second, first)
            source[:, 128 * i:128 * (i + 1)] = jnp.where(low, pick[0], pick[1]).astype(BF16)
        back = jnp.dot(table[...], source[...], preferred_element_type=F32)
        for part in range(2):
            for sh in range(2):
                start = part * modes + sh * ma * half
                levels = [back[start:start + ma * half, 128 * i:128 * (i + 1)].reshape(ma, half, 128)
                          for i in range(2)]
                send_b[(h * 2 + sh) * 2 + part, :, pair] = jnp.concatenate(levels, axis=1).astype(BF16)

    def back_send(ch):
        def send(j, carry):
            peer = ma_peer(j)
            remote(send_b.at[ch, peer], recv_b.at[ch, m], ssem_b, sem_b.at[ch], x, peer).start()
            return carry

        lax.fori_loop(0, ma - 1, send, 0)
        pltpu.make_async_copy(send_b.at[ch, m], recv_b.at[ch, m], local_b.at[ch]).start()

    ahead_chunk = functools.partial(cheb_chunk, 4)
    last_chunk = functools.partial(cheb_chunk, 0)
    lax.fori_loop(0, 4, ahead_chunk, 0)
    make_tables()
    lax.fori_loop(4, 11, ahead_chunk, 0)
    lax.fori_loop(0, 8, wait_y, 0)
    for pair in range(zd // 2):
        products(0, pair)
        if pair == 0:
            lax.fori_loop(11, 12, ahead_chunk, 0)
    lax.fori_loop(12, 16, last_chunk, 0)

    def drain(i, carry):
        back_send(i)
        wait_y(8 + 2 * i, 0)
        wait_y(9 + 2 * i, 0)
        return carry

    lax.fori_loop(0, 4, drain, 0)
    def cheb_back(more, groups, ch, carry):
        wait_received(recv_b, ch, ma - 1, sem_b, local_b)
        if more:
            back_send(ch + more)
        plane[...] = recv_b[ch].reshape(kk * half, 128).astype(F32)
        size = half // groups
        for group in range(groups):
            for s in range(group * size, (group + 1) * size, 2):
                pair = jnp.concatenate(
                    [plane[pl.ds(s + i, kk, stride=half), :] for i in range(2)], axis=1).astype(BF16)
                degrees = jnp.dot(cheb_ref[...], pair, preferred_element_type=F32).astype(BF16)
                for i in range(2):
                    send_o[ch, :, s + i] = degrees[:, 128 * i:128 * (i + 1)].reshape(nx, kd, 128)
            span = pl.ds(group * size, size)
            for j in x_order:
                remote(send_o.at[ch, x_peer(j), span], recv_o.at[ch, x, span],
                       ssem_o, sem_o.at[ch, group], x_peer(j), m).start()
        pltpu.make_async_copy(send_o.at[ch, x], recv_o.at[ch, x], local_o.at[ch]).start()
        return carry

    for pair in range(zd // 2):
        products(1, pair)
        if pair == 0:
            lax.fori_loop(0, 1, functools.partial(cheb_back, 0, 1), 0)
    back_send(4)
    back_send(5)
    lax.fori_loop(1, 3, functools.partial(cheb_back, 5, 1), 0)
    lax.fori_loop(3, 6, functools.partial(cheb_back, 0, 1), 0)
    lax.fori_loop(6, 8, functools.partial(cheb_back, 0, half // 2), 0)

    def radial_back(s, carry):
        sh = s // half
        live = count_ref[own_block * slots + s]
        rows = []
        for part in range(2):
            first, second = [], []
            for at in range(nx):
                near = recv_o[sh * 2 + part, at, s % half].astype(F32)
                far = recv_o[4 + sh * 2 + part, at, s % half].astype(F32)
                first.append(jnp.where(low, near, far).astype(BF16))
                second.append(pltpu.roll(jnp.where(low, far, near), 64, 1).astype(BF16))
            rows += [jnp.concatenate(first, axis=1), jnp.concatenate(second, axis=1)]
        values = lax.dot_general(
            jnp.concatenate(rows, axis=0), radial[s], (((1,), (1,)), ((), ())), preferred_element_type=F32)
        for part in range(2):
            for g in range(2):
                for nb in range(nbs):
                    tile = values[(part * 2 + g) * kd:(part * 2 + g + 1) * kd, 128 * nb:128 * (nb + 1)]
                    wide[pl.ds((part * nbs + nb) * 2 + g, kd, stride=row_step), :] = jnp.where(
                        lanes + nb * 128 < live, tile, 0.0)
        out_ref[s] = wide[...].astype(BF16)
        return carry

    def wait_o(ch, groups):
        own = recv_o.at[ch, x]
        pltpu.make_async_copy(own, own, local_o.at[ch]).wait()
        if groups == 1:
            wait_group(ch, 0, half)

    def wait_group(ch, group, size):
        others = recv_o.at[ch, pl.ds(0, nx - 1), pl.ds(group * size, size)]
        remote(others, others, sem_o.at[ch, group], sem_o.at[ch, group], x_peer(1), m).wait_recv()

    for ch in (0, 1, 4, 5):
        wait_o(ch, 1)
    lax.fori_loop(0, half, radial_back, 0)
    for ch in (2, 3):
        wait_o(ch, 1)
    for ch in (6, 7):
        wait_o(ch, half // 2)

    def last_slots(group, carry):
        for ch in (6, 7):
            wait_group(ch, group, 2)
        return lax.fori_loop(half + 2 * group, half + 2 * group + 2, radial_back, carry)

    lax.fori_loop(0, half // 2, last_slots, 0)

    for buffer, count, sem in (
        (recv_x, nx - 1, ssem_x), (recv_y, ma - 1, ssem_y), (recv_b, ma - 1, ssem_b), (recv_o, nx - 1, ssem_o)
    ):
        sent = buffer.at[:, pl.ds(0, count)]
        remote(sent, sent, sem, sem, x_peer(1), m).wait_send()


def body(ma_dims, forward_coef, adjoint_coef, radial_table, radial_count, mode_blocks):
    nx = lax.axis_size("zg")
    ma = lax.axis_size("ma")
    slots, kd = forward_coef.shape[:2]
    kk = nx * kd
    zd = kk // ma
    nbs = NN // 128
    coef_rows = kd * 2 * nbs * 2

    def to_rows(array):
        blocks = array.reshape(slots, kd * 2, 2, nbs, 128).transpose(0, 1, 3, 2, 4)
        return blocks.reshape(slots, coef_rows, 128)

    fourier, fourier_t, cheb, cheb_t = constant_tables()
    any_spec = pl.BlockSpec(memory_space=pl.ANY)
    vmem_spec = pl.BlockSpec(memory_space=pltpu.VMEM)
    smem_spec = pl.BlockSpec(memory_space=pltpu.SMEM)
    dma = pltpu.SemaphoreType.DMA
    rows = pl.pallas_call(
        functools.partial(kernel, (nx, ma_dims, slots, kd, zd, nbs)),
        out_shape=pltpu.VMEM((slots, coef_rows, 128), BF16),
        in_specs=[any_spec] * 5 + [vmem_spec] * 2 + [smem_spec] * 2,
        out_specs=vmem_spec,
        scratch_shapes=[
            pltpu.VMEM((2, slots, coef_rows, 128), BF16),
            pltpu.VMEM(radial_table.shape, BF16),
            pltpu.VMEM((coef_rows, 128), F32),
            pltpu.VMEM((16, nx, slots // 2, kd, 128), BF16),
            pltpu.VMEM((16, nx, slots // 2, kd, 128), BF16),
            pltpu.VMEM((16, ma, zd // 2, slots, 128), BF16),
            pltpu.VMEM((16, ma, zd // 2, slots, 128), BF16),
            pltpu.VMEM((kk * slots // 2, 128), F32),
            pltpu.VMEM((M, M), BF16),
            pltpu.VMEM((2 * M, NPHI), BF16),
            pltpu.VMEM((NPHI, 2 * M), BF16),
            pltpu.VMEM((2 * M, NPHI), BF16),
            pltpu.VMEM((NPHI, 2 * M), BF16),
            pltpu.VMEM((NPHI, 256), BF16),
            pltpu.VMEM((8, ma, zd // 2, slots, 128), BF16),
            pltpu.VMEM((8, ma, zd // 2, slots, 128), BF16),
            pltpu.VMEM((8, nx, slots // 2, kd, 128), BF16),
            pltpu.VMEM((8, nx, slots // 2, kd, 128), BF16),
            dma((2, slots)), dma((slots,)), dma((2,)),
            dma((16,)), dma((16,)), dma((8,)), dma((8,)),
            dma, dma, dma, dma,
            dma((16,)), dma((16,)), dma((8,)), dma((8, slots // 4)),
        ],
        compiler_params=pltpu.CompilerParams(
            collective_id=1, has_side_effects=True, vmem_limit_bytes=60 * 2**20
        ),
    )(to_rows(forward_coef), to_rows(adjoint_coef), radial_table, jnp.asarray(fourier), jnp.asarray(fourier_t),
      jnp.asarray(cheb), jnp.asarray(cheb_t), radial_count, mode_blocks)
    blocks = rows.reshape(slots, kd * 2, nbs, 2, 128).transpose(0, 1, 3, 2, 4)
    return blocks.reshape(forward_coef.shape)


def solution(mesh):
    placed = (P("ma", "zg", None, None, None), P("ma", "zg", None, None, None), P("ma", None, None), P(), P())
    return jax.shard_map(
        functools.partial(body, MA_DIMS), mesh=mesh, in_specs=placed,
        out_specs=P("ma", "zg", None, None, None), check_vma=False,
    )
```

```python
import functools
import math

import jax
import jax.numpy as jnp
import numpy as np
from jax import lax
from jax.experimental import pallas as pl
from jax.experimental.pallas import tpu as pltpu
from jax.sharding import PartitionSpec as P

M = 512
NN = 512
K = 128
NPHI = 1024
MA_DIMS = (4, 4, 2)
MESH = pl.DeviceIdType.MESH
BF16 = jnp.bfloat16
F32 = jnp.float32


def constant_tables():
    index = np.arange(M, dtype=np.int64)[:, None] * np.arange(NPHI, dtype=np.int64)[None, :] % NPHI
    angles = index.astype(np.float64) * (2.0 * math.pi / NPHI)
    fourier = np.concatenate([np.cos(angles), np.sin(angles)]) * math.sqrt(2.0 / NPHI)
    degree = np.arange(K, dtype=np.int64)
    cheb_index = degree[:, None] * (2 * degree[None, :] + 1) % (4 * K)
    cheb = np.cos(cheb_index.astype(np.float64) * (math.pi / (2 * K))) * math.sqrt(2.0 / K)
    fourier = fourier.astype(np.float32).astype(BF16)
    cheb = cheb.astype(np.float32).astype(BF16)
    return fourier, np.ascontiguousarray(fourier.T), cheb, np.ascontiguousarray(cheb.T)


def kernel(dims, coef0, coef1, radial_hbm, fourier_hbm, fourier_t_hbm, cheb_ref, cheb_t_ref, count_ref, block_ref,
           out_ref, coef, radial, wide, send_x, recv_x, send_y, recv_y, plane, one_hot, raw, raw_t, table, table_t,
           source, send_b, recv_b, send_o, recv_o,
           coef_sem, radial_sem, load_sem, local_x, local_y, local_b, local_o,
           ssem_x, ssem_y, ssem_b, ssem_o, sem_x, sem_y, sem_b, sem_o):
    nx, ma_dims, slots, kd, zd, nbs = dims
    ny, nz, nc = ma_dims
    ma = ny * nz * nc
    kk = nx * kd
    modes = ma * slots
    row_step = 4 * nbs
    x = lax.axis_index("zg")
    m = lax.axis_index("ma")
    my, mz, mc = m // (nz * nc), (m // nc) % nz, m % nc
    half = slots // 2
    x_order = (1,) if nx == 2 else tuple(range(2, nx - 1)) + (1, nx - 1)

    def far_first(i, n):
        return (2 + i + (i // 2) * (1 + 2 * (i % 2))) % 4 if n == 4 else n - 1 - i

    def ma_peer(j):
        dy, dz, dc = far_first(j // (nz * nc), ny), far_first((j // nc) % nz, nz), nc - 1 - j % nc
        return ((my + dy) % ny) * (nz * nc) + ((mz + dz) % nz) * nc + (mc + dc) % nc

    def x_peer(j):
        return (x + j) % nx

    peers = [ma_peer(j) for j in range(ma - 1)]

    def remote(src, dst, send_sem, recv_sem, to_x, to_m):
        return pltpu.make_async_remote_copy(
            src_ref=src, dst_ref=dst, send_sem=send_sem, recv_sem=recv_sem,
            device_id=(to_x, to_m), device_id_type=MESH,
        )

    def wait_received(buffer, ch, count, sem, local_sem):
        own = buffer.at[ch, 0]
        pltpu.make_async_copy(own, own, local_sem.at[ch]).wait()
        others = buffer.at[ch, pl.ds(0, count)]
        remote(others, others, sem.at[ch], sem.at[ch], x_peer(1), m).wait_recv()

    barrier = pltpu.get_barrier_semaphore()

    for peer in peers:
        pl.semaphore_signal(barrier, inc=1, device_id=(x, peer), device_id_type=MESH)
    for j in range(1, nx):
        pl.semaphore_signal(barrier, inc=1, device_id=(x_peer(j), m), device_id_type=MESH)

    def coef_load(arg, s):
        return pltpu.make_async_copy((coef0, coef1)[arg].at[s], coef.at[arg, s], coef_sem.at[arg, s])

    def radial_load(s):
        return pltpu.make_async_copy(radial_hbm.at[s], radial.at[s], radial_sem.at[s])

    for s in range(slots):
        coef_load(0, s).start()
        radial_load(s).start()
    for s in range(slots):
        coef_load(1, s).start()
    loads = [
        pltpu.make_async_copy(fourier_t_hbm, raw_t, load_sem.at[0]),
        pltpu.make_async_copy(fourier_hbm, raw, load_sem.at[1]),
    ]
    for load in loads:
        load.start()

    own_block = block_ref[m]
    lanes = lax.broadcasted_iota(jnp.int32, (1, 128), 1)
    low = lanes < 64

    def radial_slot(arg, s):
        coef_load(arg, s).wait()
        if arg == 0:
            radial_load(s).wait()
        live = count_ref[own_block * slots + s]
        wide[...] = coef[arg, s].astype(F32)
        rows = []
        for f in range(2):
            for part in range(2):
                tiles = []
                for nb in range(nbs):
                    tile = wide[pl.ds((part * nbs + nb) * 2 + f, kd, stride=row_step), :]
                    tiles.append(jnp.where(lanes + nb * 128 < live, tile, 0.0).astype(BF16))
                rows.append(jnp.concatenate(tiles, axis=1))
        values = jnp.dot(jnp.concatenate(rows, axis=0), radial[s], preferred_element_type=F32)
        for to in range(nx):
            first = values[:2 * kd, 128 * to:128 * (to + 1)]
            second = pltpu.roll(values[2 * kd:, 128 * to:128 * (to + 1)], 64, 1)
            halves = (jnp.where(low, first, second).astype(BF16), jnp.where(low, second, first).astype(BF16))
            for h in range(2):
                for part in range(2):
                    ch = ((h * 2 + arg) * 2 + s // half) * 2 + part
                    send_x[ch, to, s % half] = halves[h][part * kd:(part + 1) * kd]

    def x_send(ch):
        for j in x_order:
            remote(send_x.at[ch, x_peer(j)], recv_x.at[ch, x], ssem_x, sem_x.at[ch], x_peer(j), m).start()
        pltpu.make_async_copy(send_x.at[ch, x], recv_x.at[ch, x], local_x.at[ch]).start()

    def radial_first(s, carry):
        radial_slot(0, s)
        return carry

    def radial_second(s, carry):
        radial_slot(1, s)
        return carry

    lax.fori_loop(0, slots, radial_first, 0)
    pl.semaphore_wait(barrier, ma - 1 + nx - 1)
    for ch in range(4):
        x_send(ch)
    lax.fori_loop(0, slots, radial_second, 0)

    def one_hot_block(i, carry):
        part, pair = i // (ma // 2), i % (ma // 2)
        start = pl.multiple_of(i * 2 * half, 2 * half)
        column = lax.broadcasted_iota(jnp.int32, (2 * half, modes), 1)
        row = lax.broadcasted_iota(jnp.int32, (2 * half, modes), 0)
        first, second = block_ref[2 * pair] * slots, block_ref[2 * pair + 1] * slots
        mode = jnp.where(row < half, first + row, second + row - half) + part * half
        one_hot[pl.ds(start, 2 * half), :] = (column == mode).astype(F32).astype(BF16)
        return carry

    def make_tables():
        lax.fori_loop(0, ma, one_hot_block, 0)
        for load in loads:
            load.wait()
        for part in range(2):
            span = pl.ds(part * modes, modes)
            table_t[:, span] = lax.dot_general(
                raw_t[:, span], one_hot[...], (((1,), (1,)), ((), ())), preferred_element_type=F32).astype(BF16)
            table[span, :] = jnp.dot(one_hot[...], raw[span, :], preferred_element_type=F32).astype(BF16)

    def cheb_chunk(ahead, ch, carry):
        wait_received(recv_x, ch, nx - 1, sem_x, local_x)
        if ahead:
            x_send(ch + ahead)
        for s in range(0, half, 2):
            pair = jnp.concatenate([recv_x[ch, :, s + i].reshape(kk, 128) for i in range(2)], axis=1)
            levels = jnp.dot(cheb_t_ref[...], pair, preferred_element_type=F32)
            for i in range(2):
                plane[pl.ds(s + i, kk, stride=half), :] = levels[:, 128 * i:128 * (i + 1)]
        send_y[ch] = plane[...].astype(BF16).reshape(ma, zd // 2, 2 * half, 128)

        for peer in peers:
            remote(send_y.at[ch, peer], recv_y.at[ch, m], ssem_y, sem_y.at[ch], x, peer).start()
        pltpu.make_async_copy(send_y.at[ch, m], recv_y.at[ch, m], local_y.at[ch]).start()
        return carry

    def wait_y(ch, carry):
        wait_received(recv_y, ch, ma - 1, sem_y, local_y)
        return carry

    def products(h, pair):
        columns = []
        for arg in range(2):
            levels = [[], []]
            for part in range(2):
                for sh in range(2):
                    tiles = recv_y[((h * 2 + arg) * 2 + sh) * 2 + part, :, pair].astype(F32)
                    tiles = tiles.reshape(ma, 2, half, 128)
                    for i in range(2):
                        levels[i].append(tiles[:, i].reshape(ma * half, 128).astype(BF16))
            columns.append([jnp.concatenate(level, axis=0) for level in levels])
        columns = [columns[arg][i] for i in range(2) for arg in range(2)]
        grid = jnp.dot(table_t[...], jnp.concatenate(columns, axis=1), preferred_element_type=F32)
        for i in range(2):
            forward = grid[:, 256 * i:256 * i + 128]
            adjoint = grid[:, 256 * i + 128:256 * i + 256]
            straight = forward * adjoint
            crossed = forward * pltpu.roll(adjoint, 64, 1)
            first = straight + pltpu.roll(straight, 64, 1)
            second = pltpu.roll(crossed, 64, 1) - crossed
            pick = (first, second) if h == 0 else (second, first)
            source[:, 128 * i:128 * (i + 1)] = jnp.where(low, pick[0], pick[1]).astype(BF16)
        back = jnp.dot(table[...], source[...], preferred_element_type=F32)
        for part in range(2):
            for sh in range(2):
                start = part * modes + sh * ma * half
                levels = [back[start:start + ma * half, 128 * i:128 * (i + 1)].reshape(ma, half, 128)
                          for i in range(2)]
                send_b[(h * 2 + sh) * 2 + part, :, pair] = jnp.concatenate(levels, axis=1).astype(BF16)

    def back_send(ch):
        for peer in peers:
            remote(send_b.at[ch, peer], recv_b.at[ch, m], ssem_b, sem_b.at[ch], x, peer).start()
        pltpu.make_async_copy(send_b.at[ch, m], recv_b.at[ch, m], local_b.at[ch]).start()

    ahead_chunk = functools.partial(cheb_chunk, 4)
    last_chunk = functools.partial(cheb_chunk, 0)
    lax.fori_loop(0, 4, ahead_chunk, 0)
    make_tables()
    lax.fori_loop(4, 11, ahead_chunk, 0)
    lax.fori_loop(0, 8, wait_y, 0)
    for pair in range(zd // 2):
        products(0, pair)
        if pair == 0:
            lax.fori_loop(11, 12, ahead_chunk, 0)
    lax.fori_loop(12, 16, last_chunk, 0)

    def drain(i, carry):
        back_send(i)
        wait_y(8 + 2 * i, 0)
        wait_y(9 + 2 * i, 0)
        return carry

    lax.fori_loop(0, 4, drain, 0)
    def cheb_back(more, groups, ch, carry):
        wait_received(recv_b, ch, ma - 1, sem_b, local_b)
        if more:
            back_send(ch + more)
        plane[...] = recv_b[ch].reshape(kk * half, 128).astype(F32)
        size = half // groups
        for group in range(groups):
            for s in range(group * size, (group + 1) * size, 2):
                pair = jnp.concatenate(
                    [plane[pl.ds(s + i, kk, stride=half), :] for i in range(2)], axis=1).astype(BF16)
                degrees = jnp.dot(cheb_ref[...], pair, preferred_element_type=F32).astype(BF16)
                for i in range(2):
                    send_o[ch, :, s + i] = degrees[:, 128 * i:128 * (i + 1)].reshape(nx, kd, 128)
            span = pl.ds(group * size, size)
            for j in x_order:
                remote(send_o.at[ch, x_peer(j), span], recv_o.at[ch, x, span],
                       ssem_o, sem_o.at[ch, group], x_peer(j), m).start()
        pltpu.make_async_copy(send_o.at[ch, x], recv_o.at[ch, x], local_o.at[ch]).start()
        return carry

    for pair in range(zd // 2):
        products(1, pair)
        if pair == 0:
            lax.fori_loop(0, 1, functools.partial(cheb_back, 0, 1), 0)
    for ch in (4, 5):
        back_send(ch)
    lax.fori_loop(1, 3, functools.partial(cheb_back, 5, 1), 0)
    lax.fori_loop(3, 6, functools.partial(cheb_back, 0, 1), 0)
    lax.fori_loop(6, 8, functools.partial(cheb_back, 0, half // 2), 0)

    def radial_back(s, carry):
        sh = s // half
        live = count_ref[own_block * slots + s]
        rows = []
        for part in range(2):
            first, second = [], []
            for at in range(nx):
                near = recv_o[sh * 2 + part, at, s % half].astype(F32)
                far = recv_o[4 + sh * 2 + part, at, s % half].astype(F32)
                first.append(jnp.where(low, near, far).astype(BF16))
                second.append(pltpu.roll(jnp.where(low, far, near), 64, 1).astype(BF16))
            rows += [jnp.concatenate(first, axis=1), jnp.concatenate(second, axis=1)]
        values = lax.dot_general(
            jnp.concatenate(rows, axis=0), radial[s], (((1,), (1,)), ((), ())), preferred_element_type=F32)
        for part in range(2):
            for g in range(2):
                for nb in range(nbs):
                    tile = values[(part * 2 + g) * kd:(part * 2 + g + 1) * kd, 128 * nb:128 * (nb + 1)]
                    wide[pl.ds((part * nbs + nb) * 2 + g, kd, stride=row_step), :] = jnp.where(
                        lanes + nb * 128 < live, tile, 0.0)
        out_ref[s] = wide[...].astype(BF16)
        return carry

    def wait_o(ch, groups):
        own = recv_o.at[ch, x]
        pltpu.make_async_copy(own, own, local_o.at[ch]).wait()
        if groups == 1:
            wait_group(ch, 0, half)

    def wait_group(ch, group, size):
        others = recv_o.at[ch, pl.ds(0, nx - 1), pl.ds(group * size, size)]
        remote(others, others, sem_o.at[ch, group], sem_o.at[ch, group], x_peer(1), m).wait_recv()

    for ch in (0, 1, 4, 5):
        wait_o(ch, 1)
    lax.fori_loop(0, half, radial_back, 0)
    for ch in (2, 3):
        wait_o(ch, 1)
    for ch in (6, 7):
        wait_o(ch, half // 2)

    def last_slots(group, carry):
        for ch in (6, 7):
            wait_group(ch, group, 2)
        return lax.fori_loop(half + 2 * group, half + 2 * group + 2, radial_back, carry)

    lax.fori_loop(0, half // 2, last_slots, 0)

    for buffer, count, sem in (
        (recv_x, nx - 1, ssem_x), (recv_y, ma - 1, ssem_y), (recv_b, ma - 1, ssem_b), (recv_o, nx - 1, ssem_o)
    ):
        sent = buffer.at[:, pl.ds(0, count)]
        remote(sent, sent, sem, sem, x_peer(1), m).wait_send()


def body(ma_dims, forward_coef, adjoint_coef, radial_table, radial_count, mode_blocks):
    nx = lax.axis_size("zg")
    ma = lax.axis_size("ma")
    slots, kd = forward_coef.shape[:2]
    kk = nx * kd
    zd = kk // ma
    nbs = NN // 128
    coef_rows = kd * 2 * nbs * 2

    def to_rows(array):
        blocks = array.reshape(slots, kd * 2, 2, nbs, 128).transpose(0, 1, 3, 2, 4)
        return blocks.reshape(slots, coef_rows, 128)

    fourier, fourier_t, cheb, cheb_t = constant_tables()
    any_spec = pl.BlockSpec(memory_space=pl.ANY)
    vmem_spec = pl.BlockSpec(memory_space=pltpu.VMEM)
    smem_spec = pl.BlockSpec(memory_space=pltpu.SMEM)
    dma = pltpu.SemaphoreType.DMA
    rows = pl.pallas_call(
        functools.partial(kernel, (nx, ma_dims, slots, kd, zd, nbs)),
        out_shape=pltpu.VMEM((slots, coef_rows, 128), BF16),
        in_specs=[any_spec] * 5 + [vmem_spec] * 2 + [smem_spec] * 2,
        out_specs=vmem_spec,
        scratch_shapes=[
            pltpu.VMEM((2, slots, coef_rows, 128), BF16),
            pltpu.VMEM(radial_table.shape, BF16),
            pltpu.VMEM((coef_rows, 128), F32),
            pltpu.VMEM((16, nx, slots // 2, kd, 128), BF16),
            pltpu.VMEM((16, nx, slots // 2, kd, 128), BF16),
            pltpu.VMEM((16, ma, zd // 2, slots, 128), BF16),
            pltpu.VMEM((16, ma, zd // 2, slots, 128), BF16),
            pltpu.VMEM((kk * slots // 2, 128), F32),
            pltpu.VMEM((M, M), BF16),
            pltpu.VMEM((2 * M, NPHI), BF16),
            pltpu.VMEM((NPHI, 2 * M), BF16),
            pltpu.VMEM((2 * M, NPHI), BF16),
            pltpu.VMEM((NPHI, 2 * M), BF16),
            pltpu.VMEM((NPHI, 256), BF16),
            pltpu.VMEM((8, ma, zd // 2, slots, 128), BF16),
            pltpu.VMEM((8, ma, zd // 2, slots, 128), BF16),
            pltpu.VMEM((8, nx, slots // 2, kd, 128), BF16),
            pltpu.VMEM((8, nx, slots // 2, kd, 128), BF16),
            dma((2, slots)), dma((slots,)), dma((2,)),
            dma((16,)), dma((16,)), dma((8,)), dma((8,)),
            dma, dma, dma, dma,
            dma((16,)), dma((16,)), dma((8,)), dma((8, slots // 4)),
        ],
        compiler_params=pltpu.CompilerParams(
            collective_id=1, has_side_effects=True, vmem_limit_bytes=60 * 2**20
        ),
    )(to_rows(forward_coef), to_rows(adjoint_coef), radial_table, jnp.asarray(fourier), jnp.asarray(fourier_t),
      jnp.asarray(cheb), jnp.asarray(cheb_t), radial_count, mode_blocks)
    blocks = rows.reshape(slots, kd * 2, nbs, 2, 128).transpose(0, 1, 3, 2, 4)
    return blocks.reshape(forward_coef.shape)


def solution(mesh):
    placed = (P("ma", "zg", None, None, None), P("ma", "zg", None, None, None), P("ma", None, None), P(), P())
    return jax.shard_map(
        functools.partial(body, MA_DIMS), mesh=mesh, in_specs=placed,
        out_specs=P("ma", "zg", None, None, None), check_vma=False,
    )
```

```python
import functools
import math

import jax
import jax.numpy as jnp
import numpy as np
from jax import lax
from jax.experimental import pallas as pl
from jax.experimental.pallas import tpu as pltpu
from jax.sharding import PartitionSpec as P

M = 512
NN = 512
K = 128
NPHI = 1024
MA_DIMS = (4, 4, 2)
MESH = pl.DeviceIdType.MESH
BF16 = jnp.bfloat16
F32 = jnp.float32


def constant_tables():
    index = np.arange(M, dtype=np.int64)[:, None] * np.arange(NPHI, dtype=np.int64)[None, :] % NPHI
    angles = index.astype(np.float64) * (2.0 * math.pi / NPHI)
    fourier = np.concatenate([np.cos(angles), np.sin(angles)]) * math.sqrt(2.0 / NPHI)
    degree = np.arange(K, dtype=np.int64)
    cheb_index = degree[:, None] * (2 * degree[None, :] + 1) % (4 * K)
    cheb = np.cos(cheb_index.astype(np.float64) * (math.pi / (2 * K))) * math.sqrt(2.0 / K)
    fourier = fourier.astype(np.float32).astype(BF16)
    cheb = cheb.astype(np.float32).astype(BF16)
    return fourier, np.ascontiguousarray(fourier.T), cheb, np.ascontiguousarray(cheb.T)


def kernel(dims, coef0, coef1, radial_hbm, fourier_hbm, fourier_t_hbm, cheb_ref, cheb_t_ref, count_ref, block_ref,
           out_ref, coef, radial, wide, send_x, recv_x, send_y, recv_y, plane, one_hot, raw, raw_t, table, table_t,
           grid0, source, send_b, recv_b, send_o, recv_o,
           coef_sem, radial_sem, load_sem, local_x, local_y, local_b, local_o,
           ssem_x, ssem_y, ssem_b, ssem_o, sem_x, sem_y, sem_b, sem_o):
    nx, ma_dims, slots, kd, zd, nbs = dims
    ny, nz, nc = ma_dims
    ma = ny * nz * nc
    kk = nx * kd
    modes = ma * slots
    row_step = 4 * nbs
    x = lax.axis_index("zg")
    m = lax.axis_index("ma")
    my, mz, mc = m // (nz * nc), (m // nc) % nz, m % nc
    half = slots // 2
    x_order = (1,) if nx == 2 else tuple(range(2, nx - 1)) + (1, nx - 1)

    def far_first(i, n):
        return (2 + i + (i // 2) * (1 + 2 * (i % 2))) % 4 if n == 4 else n - 1 - i

    def ma_peer(j):
        dy, dz, dc = far_first(j // (nz * nc), ny), far_first((j // nc) % nz, nz), nc - 1 - j % nc
        return ((my + dy) % ny) * (nz * nc) + ((mz + dz) % nz) * nc + (mc + dc) % nc

    def x_peer(j):
        return (x + j) % nx

    peers = [ma_peer(j) for j in range(ma - 1)]

    def remote(src, dst, send_sem, recv_sem, to_x, to_m):
        return pltpu.make_async_remote_copy(
            src_ref=src, dst_ref=dst, send_sem=send_sem, recv_sem=recv_sem,
            device_id=(to_x, to_m), device_id_type=MESH,
        )

    def wait_received(buffer, ch, count, sem, local_sem):
        own = buffer.at[ch, 0]
        pltpu.make_async_copy(own, own, local_sem.at[ch]).wait()
        others = buffer.at[ch, pl.ds(0, count)]
        remote(others, others, sem.at[ch], sem.at[ch], x_peer(1), m).wait_recv()

    barrier = pltpu.get_barrier_semaphore()

    for peer in peers:
        pl.semaphore_signal(barrier, inc=1, device_id=(x, peer), device_id_type=MESH)
    for j in range(1, nx):
        pl.semaphore_signal(barrier, inc=1, device_id=(x_peer(j), m), device_id_type=MESH)

    def coef_load(arg, s):
        return pltpu.make_async_copy((coef0, coef1)[arg].at[s], coef.at[arg, s], coef_sem.at[arg, s])

    def radial_load(s):
        return pltpu.make_async_copy(radial_hbm.at[s], radial.at[s], radial_sem.at[s])

    for s in range(slots):
        coef_load(0, s).start()
        radial_load(s).start()
    for s in range(slots):
        coef_load(1, s).start()
    loads = [
        pltpu.make_async_copy(fourier_t_hbm, raw_t, load_sem.at[0]),
        pltpu.make_async_copy(fourier_hbm, raw, load_sem.at[1]),
    ]
    for load in loads:
        load.start()

    own_block = block_ref[m]
    lanes = lax.broadcasted_iota(jnp.int32, (1, 128), 1)
    low = lanes < 64

    def radial_slot(arg, s):
        coef_load(arg, s).wait()
        if arg == 0:
            radial_load(s).wait()
        live = count_ref[own_block * slots + s]
        wide[...] = coef[arg, s].astype(F32)
        rows = []
        for f in range(2):
            for part in range(2):
                tiles = []
                for nb in range(nbs):
                    tile = wide[pl.ds((part * nbs + nb) * 2 + f, kd, stride=row_step), :]
                    tiles.append(jnp.where(lanes + nb * 128 < live, tile, 0.0).astype(BF16))
                rows.append(jnp.concatenate(tiles, axis=1))
        values = jnp.dot(jnp.concatenate(rows, axis=0), radial[s], preferred_element_type=F32)
        for to in range(nx):
            first = values[:2 * kd, 128 * to:128 * (to + 1)]
            second = pltpu.roll(values[2 * kd:, 128 * to:128 * (to + 1)], 64, 1)
            halves = (jnp.where(low, first, second).astype(BF16), jnp.where(low, second, first).astype(BF16))
            for h in range(2):
                for part in range(2):
                    ch = ((h * 2 + arg) * 2 + s // half) * 2 + part
                    send_x[ch, to, s % half] = halves[h][part * kd:(part + 1) * kd]

    def x_send(ch):
        for j in x_order:
            remote(send_x.at[ch, x_peer(j)], recv_x.at[ch, x], ssem_x, sem_x.at[ch], x_peer(j), m).start()
        pltpu.make_async_copy(send_x.at[ch, x], recv_x.at[ch, x], local_x.at[ch]).start()

    def radial_first(s, carry):
        radial_slot(0, s)
        return carry

    def radial_second(s, carry):
        radial_slot(1, s)
        return carry

    lax.fori_loop(0, slots, radial_first, 0)
    pl.semaphore_wait(barrier, ma - 1 + nx - 1)
    for ch in range(4):
        x_send(ch)
    lax.fori_loop(0, slots, radial_second, 0)

    def one_hot_block(i, carry):
        part, pair = i // (ma // 2), i % (ma // 2)
        start = pl.multiple_of(i * 2 * half, 2 * half)
        column = lax.broadcasted_iota(jnp.int32, (2 * half, modes), 1)
        row = lax.broadcasted_iota(jnp.int32, (2 * half, modes), 0)
        first, second = block_ref[2 * pair] * slots, block_ref[2 * pair + 1] * slots
        mode = jnp.where(row < half, first + row, second + row - half) + part * half
        one_hot[pl.ds(start, 2 * half), :] = (column == mode).astype(F32).astype(BF16)
        return carry

    def make_tables():
        lax.fori_loop(0, ma, one_hot_block, 0)
        for load in loads:
            load.wait()
        for part in range(2):
            span = pl.ds(part * modes, modes)
            table_t[:, span] = lax.dot_general(
                raw_t[:, span], one_hot[...], (((1,), (1,)), ((), ())), preferred_element_type=F32).astype(BF16)
            table[span, :] = jnp.dot(one_hot[...], raw[span, :], preferred_element_type=F32).astype(BF16)

    def cheb_chunk(ahead, ch, carry):
        wait_received(recv_x, ch, nx - 1, sem_x, local_x)
        if ahead:
            x_send(ch + ahead)
        for s in range(0, half, 2):
            pair = jnp.concatenate([recv_x[ch, :, s + i].reshape(kk, 128) for i in range(2)], axis=1)
            levels = jnp.dot(cheb_t_ref[...], pair, preferred_element_type=F32)
            for i in range(2):
                plane[pl.ds(s + i, kk, stride=half), :] = levels[:, 128 * i:128 * (i + 1)]
        send_y[ch] = plane[...].astype(BF16).reshape(ma, zd // 2, 2 * half, 128)

        for peer in peers:
            remote(send_y.at[ch, peer], recv_y.at[ch, m], ssem_y, sem_y.at[ch], x, peer).start()
        pltpu.make_async_copy(send_y.at[ch, m], recv_y.at[ch, m], local_y.at[ch]).start()
        return carry

    def wait_y(ch, carry):
        wait_received(recv_y, ch, ma - 1, sem_y, local_y)
        return carry

    def synthesis(h, arg, pair):
        levels = [[], []]
        for part in range(2):
            for sh in range(2):
                tiles = recv_y[((h * 2 + arg) * 2 + sh) * 2 + part, :, pair].astype(F32)
                tiles = tiles.reshape(ma, 2, half, 128)
                for i in range(2):
                    levels[i].append(tiles[:, i].reshape(ma * half, 128).astype(BF16))
        columns = jnp.concatenate([jnp.concatenate(level, axis=0) for level in levels], axis=1)
        return jnp.dot(table_t[...], columns, preferred_element_type=F32)

    def forward_grids(h):
        for pair in range(zd // 2):
            grid0[pair] = synthesis(h, 0, pair)

    def products(h, pair):
        grid = synthesis(h, 1, pair)
        for i in range(2):
            forward = grid0[pair, :, 128 * i:128 * (i + 1)]
            adjoint = grid[:, 128 * i:128 * (i + 1)]
            straight = forward * adjoint
            crossed = forward * pltpu.roll(adjoint, 64, 1)
            first = straight + pltpu.roll(straight, 64, 1)
            second = pltpu.roll(crossed, 64, 1) - crossed
            pick = (first, second) if h == 0 else (second, first)
            source[:, 128 * i:128 * (i + 1)] = jnp.where(low, pick[0], pick[1]).astype(BF16)
        back = jnp.dot(table[...], source[...], preferred_element_type=F32)
        for part in range(2):
            for sh in range(2):
                start = part * modes + sh * ma * half
                levels = [back[start:start + ma * half, 128 * i:128 * (i + 1)].reshape(ma, half, 128)
                          for i in range(2)]
                send_b[(h * 2 + sh) * 2 + part, :, pair] = jnp.concatenate(levels, axis=1).astype(BF16)

    def back_send(ch):
        for peer in peers:
            remote(send_b.at[ch, peer], recv_b.at[ch, m], ssem_b, sem_b.at[ch], x, peer).start()
        pltpu.make_async_copy(send_b.at[ch, m], recv_b.at[ch, m], local_b.at[ch]).start()

    ahead_chunk = functools.partial(cheb_chunk, 4)
    last_chunk = functools.partial(cheb_chunk, 0)
    lax.fori_loop(0, 4, ahead_chunk, 0)
    make_tables()
    lax.fori_loop(4, 8, ahead_chunk, 0)
    lax.fori_loop(0, 4, wait_y, 0)
    forward_grids(0)
    lax.fori_loop(8, 11, ahead_chunk, 0)
    lax.fori_loop(4, 8, wait_y, 0)
    for pair in range(zd // 2):
        products(0, pair)
        if pair == 0:
            lax.fori_loop(11, 12, ahead_chunk, 0)
    lax.fori_loop(12, 15, last_chunk, 0)
    lax.fori_loop(8, 12, wait_y, 0)
    forward_grids(1)
    lax.fori_loop(15, 16, last_chunk, 0)

    def drain(i, carry):
        back_send(i)
        wait_y(12 + i, 0)
        return carry

    lax.fori_loop(0, 4, drain, 0)
    def cheb_back(more, groups, ch, carry):
        wait_received(recv_b, ch, ma - 1, sem_b, local_b)
        if more:
            back_send(ch + more)
        plane[...] = recv_b[ch].reshape(kk * half, 128).astype(F32)
        size = half // groups
        for group in range(groups):
            for s in range(group * size, (group + 1) * size, 2):
                pair = jnp.concatenate(
                    [plane[pl.ds(s + i, kk, stride=half), :] for i in range(2)], axis=1).astype(BF16)
                degrees = jnp.dot(cheb_ref[...], pair, preferred_element_type=F32).astype(BF16)
                for i in range(2):
                    send_o[ch, :, s + i] = degrees[:, 128 * i:128 * (i + 1)].reshape(nx, kd, 128)
            span = pl.ds(group * size, size)
            for j in x_order:
                remote(send_o.at[ch, x_peer(j), span], recv_o.at[ch, x, span],
                       ssem_o, sem_o.at[ch, group], x_peer(j), m).start()
        pltpu.make_async_copy(send_o.at[ch, x], recv_o.at[ch, x], local_o.at[ch]).start()
        return carry

    for pair in range(zd // 2):
        products(1, pair)
        if pair == 0:
            lax.fori_loop(0, 1, functools.partial(cheb_back, 0, 1), 0)
    for ch in (4, 5):
        back_send(ch)
    lax.fori_loop(1, 3, functools.partial(cheb_back, 5, 1), 0)
    lax.fori_loop(3, 6, functools.partial(cheb_back, 0, 1), 0)
    lax.fori_loop(6, 8, functools.partial(cheb_back, 0, half // 2), 0)

    def radial_back(s, carry):
        sh = s // half
        live = count_ref[own_block * slots + s]
        rows = []
        for part in range(2):
            first, second = [], []
            for at in range(nx):
                near = recv_o[sh * 2 + part, at, s % half].astype(F32)
                far = recv_o[4 + sh * 2 + part, at, s % half].astype(F32)
                first.append(jnp.where(low, near, far).astype(BF16))
                second.append(pltpu.roll(jnp.where(low, far, near), 64, 1).astype(BF16))
            rows += [jnp.concatenate(first, axis=1), jnp.concatenate(second, axis=1)]
        values = lax.dot_general(
            jnp.concatenate(rows, axis=0), radial[s], (((1,), (1,)), ((), ())), preferred_element_type=F32)
        for part in range(2):
            for g in range(2):
                for nb in range(nbs):
                    tile = values[(part * 2 + g) * kd:(part * 2 + g + 1) * kd, 128 * nb:128 * (nb + 1)]
                    wide[pl.ds((part * nbs + nb) * 2 + g, kd, stride=row_step), :] = jnp.where(
                        lanes + nb * 128 < live, tile, 0.0)
        out_ref[s] = wide[...].astype(BF16)
        return carry

    def wait_o(ch, groups):
        own = recv_o.at[ch, x]
        pltpu.make_async_copy(own, own, local_o.at[ch]).wait()
        if groups == 1:
            wait_group(ch, 0, half)

    def wait_group(ch, group, size):
        others = recv_o.at[ch, pl.ds(0, nx - 1), pl.ds(group * size, size)]
        remote(others, others, sem_o.at[ch, group], sem_o.at[ch, group], x_peer(1), m).wait_recv()

    for ch in (0, 1, 4, 5):
        wait_o(ch, 1)
    lax.fori_loop(0, half, radial_back, 0)
    for ch in (2, 3):
        wait_o(ch, 1)
    for ch in (6, 7):
        wait_o(ch, half // 2)

    def last_slots(group, carry):
        for ch in (6, 7):
            wait_group(ch, group, 2)
        return lax.fori_loop(half + 2 * group, half + 2 * group + 2, radial_back, carry)

    lax.fori_loop(0, half // 2, last_slots, 0)

    for buffer, count, sem in (
        (recv_x, nx - 1, ssem_x), (recv_y, ma - 1, ssem_y), (recv_b, ma - 1, ssem_b), (recv_o, nx - 1, ssem_o)
    ):
        sent = buffer.at[:, pl.ds(0, count)]
        remote(sent, sent, sem, sem, x_peer(1), m).wait_send()


def body(ma_dims, forward_coef, adjoint_coef, radial_table, radial_count, mode_blocks):
    nx = lax.axis_size("zg")
    ma = lax.axis_size("ma")
    slots, kd = forward_coef.shape[:2]
    kk = nx * kd
    zd = kk // ma
    nbs = NN // 128
    coef_rows = kd * 2 * nbs * 2

    def to_rows(array):
        blocks = array.reshape(slots, kd * 2, 2, nbs, 128).transpose(0, 1, 3, 2, 4)
        return blocks.reshape(slots, coef_rows, 128)

    fourier, fourier_t, cheb, cheb_t = constant_tables()
    any_spec = pl.BlockSpec(memory_space=pl.ANY)
    vmem_spec = pl.BlockSpec(memory_space=pltpu.VMEM)
    smem_spec = pl.BlockSpec(memory_space=pltpu.SMEM)
    dma = pltpu.SemaphoreType.DMA
    rows = pl.pallas_call(
        functools.partial(kernel, (nx, ma_dims, slots, kd, zd, nbs)),
        out_shape=pltpu.VMEM((slots, coef_rows, 128), BF16),
        in_specs=[any_spec] * 5 + [vmem_spec] * 2 + [smem_spec] * 2,
        out_specs=vmem_spec,
        scratch_shapes=[
            pltpu.VMEM((2, slots, coef_rows, 128), BF16),
            pltpu.VMEM(radial_table.shape, BF16),
            pltpu.VMEM((coef_rows, 128), F32),
            pltpu.VMEM((16, nx, slots // 2, kd, 128), BF16),
            pltpu.VMEM((16, nx, slots // 2, kd, 128), BF16),
            pltpu.VMEM((16, ma, zd // 2, slots, 128), BF16),
            pltpu.VMEM((16, ma, zd // 2, slots, 128), BF16),
            pltpu.VMEM((kk * slots // 2, 128), F32),
            pltpu.VMEM((M, M), BF16),
            pltpu.VMEM((2 * M, NPHI), BF16),
            pltpu.VMEM((NPHI, 2 * M), BF16),
            pltpu.VMEM((2 * M, NPHI), BF16),
            pltpu.VMEM((NPHI, 2 * M), BF16),
            pltpu.VMEM((zd // 2, NPHI, 256), F32),
            pltpu.VMEM((NPHI, 256), BF16),
            pltpu.VMEM((8, ma, zd // 2, slots, 128), BF16),
            pltpu.VMEM((8, ma, zd // 2, slots, 128), BF16),
            pltpu.VMEM((8, nx, slots // 2, kd, 128), BF16),
            pltpu.VMEM((8, nx, slots // 2, kd, 128), BF16),
            dma((2, slots)), dma((slots,)), dma((2,)),
            dma((16,)), dma((16,)), dma((8,)), dma((8,)),
            dma, dma, dma, dma,
            dma((16,)), dma((16,)), dma((8,)), dma((8, slots // 4)),
        ],
        compiler_params=pltpu.CompilerParams(
            collective_id=1, has_side_effects=True, vmem_limit_bytes=60 * 2**20
        ),
    )(to_rows(forward_coef), to_rows(adjoint_coef), radial_table, jnp.asarray(fourier), jnp.asarray(fourier_t),
      jnp.asarray(cheb), jnp.asarray(cheb_t), radial_count, mode_blocks)
    blocks = rows.reshape(slots, kd * 2, nbs, 2, 128).transpose(0, 1, 3, 2, 4)
    return blocks.reshape(forward_coef.shape)


def solution(mesh):
    placed = (P("ma", "zg", None, None, None), P("ma", "zg", None, None, None), P("ma", None, None), P(), P())
    return jax.shard_map(
        functools.partial(body, MA_DIMS), mesh=mesh, in_specs=placed,
        out_specs=P("ma", "zg", None, None, None), check_vma=False,
    )
```

```python
import functools
import math

import jax
import jax.numpy as jnp
import numpy as np
from jax import lax
from jax.experimental import pallas as pl
from jax.experimental.pallas import tpu as pltpu
from jax.sharding import PartitionSpec as P

M = 512
NN = 512
K = 128
NPHI = 1024
MA_DIMS = (4, 4, 2)
MESH = pl.DeviceIdType.MESH
BF16 = jnp.bfloat16
F32 = jnp.float32


def constant_tables():
    index = np.arange(M, dtype=np.int64)[:, None] * np.arange(NPHI, dtype=np.int64)[None, :] % NPHI
    angles = index.astype(np.float64) * (2.0 * math.pi / NPHI)
    fourier = np.concatenate([np.cos(angles), np.sin(angles)]) * math.sqrt(2.0 / NPHI)
    degree = np.arange(K, dtype=np.int64)
    cheb_index = degree[:, None] * (2 * degree[None, :] + 1) % (4 * K)
    cheb = np.cos(cheb_index.astype(np.float64) * (math.pi / (2 * K))) * math.sqrt(2.0 / K)
    fourier = fourier.astype(np.float32).astype(BF16)
    cheb = cheb.astype(np.float32).astype(BF16)
    return fourier, np.ascontiguousarray(fourier.T), cheb, np.ascontiguousarray(cheb.T)


def kernel(dims, coef0, coef1, radial_hbm, fourier_hbm, fourier_t_hbm, cheb_ref, cheb_t_ref, count_ref, block_ref,
           out_ref, coef, radial, wide, send_x, recv_x, send_y, recv_y, plane, one_hot, raw, raw_t, table, table_t,
           grid0, source, send_b, recv_b, send_o, recv_o,
           coef_sem, radial_sem, load_sem, local_x, local_y, local_b, local_o,
           ssem_x, ssem_y, ssem_b, ssem_o, sem_x, sem_y, sem_b, sem_o):
    nx, ma_dims, slots, kd, zd, nbs = dims
    ny, nz, nc = ma_dims
    ma = ny * nz * nc
    kk = nx * kd
    modes = ma * slots
    row_step = 4 * nbs
    x = lax.axis_index("zg")
    m = lax.axis_index("ma")
    my, mz, mc = m // (nz * nc), (m // nc) % nz, m % nc
    half = slots // 2
    x_order = (1,) if nx == 2 else tuple(range(2, nx - 1)) + (1, nx - 1)

    def far_first(i, n):
        return (2 + i + (i // 2) * (1 + 2 * (i % 2))) % 4 if n == 4 else n - 1 - i

    def ma_peer(j):
        dy, dz, dc = far_first(j // (nz * nc), ny), far_first((j // nc) % nz, nz), nc - 1 - j % nc
        return ((my + dy) % ny) * (nz * nc) + ((mz + dz) % nz) * nc + (mc + dc) % nc

    def x_peer(j):
        return (x + j) % nx

    peers = [ma_peer(j) for j in range(ma - 1)]

    def remote(src, dst, send_sem, recv_sem, to_x, to_m):
        return pltpu.make_async_remote_copy(
            src_ref=src, dst_ref=dst, send_sem=send_sem, recv_sem=recv_sem,
            device_id=(to_x, to_m), device_id_type=MESH,
        )

    def wait_received(buffer, ch, count, sem, local_sem):
        own = buffer.at[ch, 0]
        pltpu.make_async_copy(own, own, local_sem.at[ch]).wait()
        others = buffer.at[ch, pl.ds(0, count)]
        remote(others, others, sem.at[ch], sem.at[ch], x_peer(1), m).wait_recv()

    barrier = pltpu.get_barrier_semaphore()

    for peer in peers:
        pl.semaphore_signal(barrier, inc=1, device_id=(x, peer), device_id_type=MESH)
    for j in range(1, nx):
        pl.semaphore_signal(barrier, inc=1, device_id=(x_peer(j), m), device_id_type=MESH)

    def coef_load(arg, s):
        return pltpu.make_async_copy((coef0, coef1)[arg].at[s], coef.at[arg, s], coef_sem.at[arg, s])

    def radial_load(s):
        return pltpu.make_async_copy(radial_hbm.at[s], radial.at[s], radial_sem.at[s])

    for s in range(slots):
        coef_load(0, s).start()
        radial_load(s).start()
    for s in range(slots):
        coef_load(1, s).start()
    loads = [
        pltpu.make_async_copy(fourier_t_hbm, raw_t, load_sem.at[0]),
        pltpu.make_async_copy(fourier_hbm, raw, load_sem.at[1]),
    ]
    for load in loads:
        load.start()

    own_block = block_ref[m]
    lanes = lax.broadcasted_iota(jnp.int32, (1, 128), 1)
    low = lanes < 64

    def radial_slot(arg, s):
        coef_load(arg, s).wait()
        if arg == 0:
            radial_load(s).wait()
        live = count_ref[own_block * slots + s]
        wide[...] = coef[arg, s].astype(F32)
        rows = []
        for f in range(2):
            for part in range(2):
                tiles = []
                for nb in range(nbs):
                    tile = wide[pl.ds((part * nbs + nb) * 2 + f, kd, stride=row_step), :]
                    tiles.append(jnp.where(lanes + nb * 128 < live, tile, 0.0).astype(BF16))
                rows.append(jnp.concatenate(tiles, axis=1))
        values = jnp.dot(jnp.concatenate(rows, axis=0), radial[s], preferred_element_type=F32)
        for to in range(nx):
            first = values[:2 * kd, 128 * to:128 * (to + 1)]
            second = pltpu.roll(values[2 * kd:, 128 * to:128 * (to + 1)], 64, 1)
            halves = (jnp.where(low, first, second).astype(BF16), jnp.where(low, second, first).astype(BF16))
            for h in range(2):
                for part in range(2):
                    ch = ((h * 2 + arg) * 2 + s // half) * 2 + part
                    send_x[ch, to, s % half] = halves[h][part * kd:(part + 1) * kd]

    def x_send(ch):
        for j in x_order:
            remote(send_x.at[ch, x_peer(j)], recv_x.at[ch, x], ssem_x, sem_x.at[ch], x_peer(j), m).start()
        pltpu.make_async_copy(send_x.at[ch, x], recv_x.at[ch, x], local_x.at[ch]).start()

    def radial_first(s, carry):
        radial_slot(0, s)
        return carry

    def radial_second(s, carry):
        radial_slot(1, s)
        return carry

    lax.fori_loop(0, slots, radial_first, 0)
    pl.semaphore_wait(barrier, ma - 1 + nx - 1)
    for ch in range(4):
        x_send(ch)
    lax.fori_loop(0, slots, radial_second, 0)

    def one_hot_block(i, carry):
        part, pair = i // (ma // 2), i % (ma // 2)
        start = pl.multiple_of(i * 2 * half, 2 * half)
        column = lax.broadcasted_iota(jnp.int32, (2 * half, modes), 1)
        row = lax.broadcasted_iota(jnp.int32, (2 * half, modes), 0)
        first, second = block_ref[2 * pair] * slots, block_ref[2 * pair + 1] * slots
        mode = jnp.where(row < half, first + row, second + row - half) + part * half
        one_hot[pl.ds(start, 2 * half), :] = (column == mode).astype(F32).astype(BF16)
        return carry

    def make_tables():
        lax.fori_loop(0, ma, one_hot_block, 0)
        for load in loads:
            load.wait()
        for part in range(2):
            span = pl.ds(part * modes, modes)
            table_t[:, span] = lax.dot_general(
                raw_t[:, span], one_hot[...], (((1,), (1,)), ((), ())), preferred_element_type=F32).astype(BF16)
            table[span, :] = jnp.dot(one_hot[...], raw[span, :], preferred_element_type=F32).astype(BF16)

    def cheb_chunk(ahead, ch, carry):
        wait_received(recv_x, ch, nx - 1, sem_x, local_x)
        if ahead:
            x_send(ch + ahead)
        for s in range(0, half, 2):
            pair = jnp.concatenate([recv_x[ch, :, s + i].reshape(kk, 128) for i in range(2)], axis=1)
            levels = jnp.dot(cheb_t_ref[...], pair, preferred_element_type=F32)
            for i in range(2):
                plane[pl.ds(s + i, kk, stride=half), :] = levels[:, 128 * i:128 * (i + 1)]
        send_y[ch] = plane[...].astype(BF16).reshape(ma, zd // 2, 2 * half, 128)

        for peer in peers:
            remote(send_y.at[ch, peer], recv_y.at[ch, m], ssem_y, sem_y.at[ch], x, peer).start()
        pltpu.make_async_copy(send_y.at[ch, m], recv_y.at[ch, m], local_y.at[ch]).start()
        return carry

    def wait_y(ch, carry):
        wait_received(recv_y, ch, ma - 1, sem_y, local_y)
        return carry

    def synthesis(h, arg, pair):
        levels = [[], []]
        for part in range(2):
            for sh in range(2):
                tiles = recv_y[((h * 2 + arg) * 2 + sh) * 2 + part, :, pair].astype(F32)
                tiles = tiles.reshape(ma, 2, half, 128)
                for i in range(2):
                    levels[i].append(tiles[:, i].reshape(ma * half, 128).astype(BF16))
        columns = jnp.concatenate([jnp.concatenate(level, axis=0) for level in levels], axis=1)
        return jnp.dot(table_t[...], columns, preferred_element_type=F32)

    def forward_grids(h):
        for pair in range(zd // 2):
            grid0[pair] = synthesis(h, 0, pair)

    def products(h, pair):
        grid = synthesis(h, 1, pair)
        for i in range(2):
            forward = grid0[pair, :, 128 * i:128 * (i + 1)]
            adjoint = grid[:, 128 * i:128 * (i + 1)]
            straight = forward * adjoint
            crossed = forward * pltpu.roll(adjoint, 64, 1)
            first = straight + pltpu.roll(straight, 64, 1)
            second = pltpu.roll(crossed, 64, 1) - crossed
            pick = (first, second) if h == 0 else (second, first)
            source[:, 128 * i:128 * (i + 1)] = jnp.where(low, pick[0], pick[1]).astype(BF16)
        back = jnp.dot(table[...], source[...], preferred_element_type=F32)
        for part in range(2):
            for sh in range(2):
                start = part * modes + sh * ma * half
                levels = [back[start:start + ma * half, 128 * i:128 * (i + 1)].reshape(ma, half, 128)
                          for i in range(2)]
                send_b[(h * 2 + sh) * 2 + part, :, pair] = jnp.concatenate(levels, axis=1).astype(BF16)

    def back_send(ch):
        for peer in peers:
            remote(send_b.at[ch, peer], recv_b.at[ch, m], ssem_b, sem_b.at[ch], x, peer).start()
        pltpu.make_async_copy(send_b.at[ch, m], recv_b.at[ch, m], local_b.at[ch]).start()

    ahead_chunk = functools.partial(cheb_chunk, 4)
    last_chunk = functools.partial(cheb_chunk, 0)
    lax.fori_loop(0, 4, ahead_chunk, 0)
    make_tables()
    lax.fori_loop(4, 8, ahead_chunk, 0)
    lax.fori_loop(0, 4, wait_y, 0)
    forward_grids(0)
    lax.fori_loop(8, 11, ahead_chunk, 0)
    lax.fori_loop(4, 8, wait_y, 0)
    for pair in range(zd // 2):
        products(0, pair)
        if pair == 0:
            lax.fori_loop(11, 12, ahead_chunk, 0)
    lax.fori_loop(12, 15, last_chunk, 0)
    lax.fori_loop(8, 12, wait_y, 0)
    forward_grids(1)
    lax.fori_loop(15, 16, last_chunk, 0)

    def drain(i, carry):
        back_send(i)
        wait_y(12 + i, 0)
        return carry

    lax.fori_loop(0, 4, drain, 0)
    def cheb_back(more, groups, ch, carry):
        wait_received(recv_b, ch, ma - 1, sem_b, local_b)
        if more:
            back_send(ch + more)
        plane[...] = recv_b[ch].reshape(kk * half, 128).astype(F32)
        size = half // groups
        for group in range(groups):
            for s in range(group * size, (group + 1) * size, 2):
                pair = jnp.concatenate(
                    [plane[pl.ds(s + i, kk, stride=half), :] for i in range(2)], axis=1).astype(BF16)
                degrees = jnp.dot(cheb_ref[...], pair, preferred_element_type=F32).astype(BF16)
                for i in range(2):
                    send_o[ch, :, s + i] = degrees[:, 128 * i:128 * (i + 1)].reshape(nx, kd, 128)
            span = pl.ds(group * size, size)
            for j in x_order:
                remote(send_o.at[ch, x_peer(j), span], recv_o.at[ch, x, span],
                       ssem_o, sem_o.at[ch, group], x_peer(j), m).start()
        pltpu.make_async_copy(send_o.at[ch, x], recv_o.at[ch, x], local_o.at[ch]).start()
        return carry

    for pair in range(zd // 2):
        products(1, pair)
        if pair == 0:
            lax.fori_loop(0, 1, functools.partial(cheb_back, 0, 1), 0)
    for ch in (4, 5):
        back_send(ch)
    lax.fori_loop(1, 3, functools.partial(cheb_back, 5, 1), 0)
    lax.fori_loop(3, 6, functools.partial(cheb_back, 0, 1), 0)
    lax.fori_loop(6, 8, functools.partial(cheb_back, 0, half // 2), 0)

    def radial_back(s, base):
        sh = s // half
        live = count_ref[own_block * slots + s]
        rows = []
        for part in range(2):
            first, second = [], []
            for at in range(nx):
                near = recv_o[sh * 2 + part, at, s % half].astype(F32)
                far = recv_o[4 + sh * 2 + part, at, s % half].astype(F32)
                first.append(jnp.where(low, near, far).astype(BF16))
                second.append(pltpu.roll(jnp.where(low, far, near), 64, 1).astype(BF16))
            rows += [jnp.concatenate(first, axis=1), jnp.concatenate(second, axis=1)]
        values = lax.dot_general(
            jnp.concatenate(rows, axis=0), radial[s], (((1,), (1,)), ((), ())), preferred_element_type=F32)
        for part in range(2):
            for g in range(2):
                for nb in range(nbs):
                    tile = values[(part * 2 + g) * kd:(part * 2 + g + 1) * kd, 128 * nb:128 * (nb + 1)]
                    plane[pl.ds(base + (part * nbs + nb) * 2 + g, kd, stride=row_step), :] = jnp.where(
                        lanes + nb * 128 < live, tile, 0.0)
        out_ref[s] = plane[pl.ds(base, 2 * nbs * 2 * kd), :].astype(BF16)

    def radial_pair(i, carry):
        for k in range(2):
            radial_back(2 * i + k, k * 2 * nbs * 2 * kd)
        return carry

    def wait_o(ch, groups):
        own = recv_o.at[ch, x]
        pltpu.make_async_copy(own, own, local_o.at[ch]).wait()
        if groups == 1:
            wait_group(ch, 0, half)

    def wait_group(ch, group, size):
        others = recv_o.at[ch, pl.ds(0, nx - 1), pl.ds(group * size, size)]
        remote(others, others, sem_o.at[ch, group], sem_o.at[ch, group], x_peer(1), m).wait_recv()

    for ch in (0, 1, 4, 5):
        wait_o(ch, 1)
    lax.fori_loop(0, half // 2, radial_pair, 0)
    for ch in (2, 3):
        wait_o(ch, 1)
    for ch in (6, 7):
        wait_o(ch, half // 2)

    def last_slots(group, carry):
        for ch in (6, 7):
            wait_group(ch, group, 2)
        return radial_pair(half // 2 + group, carry)

    lax.fori_loop(0, half // 2, last_slots, 0)

    for buffer, count, sem in (
        (recv_x, nx - 1, ssem_x), (recv_y, ma - 1, ssem_y), (recv_b, ma - 1, ssem_b), (recv_o, nx - 1, ssem_o)
    ):
        sent = buffer.at[:, pl.ds(0, count)]
        remote(sent, sent, sem, sem, x_peer(1), m).wait_send()


def body(ma_dims, forward_coef, adjoint_coef, radial_table, radial_count, mode_blocks):
    nx = lax.axis_size("zg")
    ma = lax.axis_size("ma")
    slots, kd = forward_coef.shape[:2]
    kk = nx * kd
    zd = kk // ma
    nbs = NN // 128
    coef_rows = kd * 2 * nbs * 2

    def to_rows(array):
        blocks = array.reshape(slots, kd * 2, 2, nbs, 128).transpose(0, 1, 3, 2, 4)
        return blocks.reshape(slots, coef_rows, 128)

    fourier, fourier_t, cheb, cheb_t = constant_tables()
    any_spec = pl.BlockSpec(memory_space=pl.ANY)
    vmem_spec = pl.BlockSpec(memory_space=pltpu.VMEM)
    smem_spec = pl.BlockSpec(memory_space=pltpu.SMEM)
    dma = pltpu.SemaphoreType.DMA
    rows = pl.pallas_call(
        functools.partial(kernel, (nx, ma_dims, slots, kd, zd, nbs)),
        out_shape=pltpu.VMEM((slots, coef_rows, 128), BF16),
        in_specs=[any_spec] * 5 + [vmem_spec] * 2 + [smem_spec] * 2,
        out_specs=vmem_spec,
        scratch_shapes=[
            pltpu.VMEM((2, slots, coef_rows, 128), BF16),
            pltpu.VMEM(radial_table.shape, BF16),
            pltpu.VMEM((coef_rows, 128), F32),
            pltpu.VMEM((16, nx, slots // 2, kd, 128), BF16),
            pltpu.VMEM((16, nx, slots // 2, kd, 128), BF16),
            pltpu.VMEM((16, ma, zd // 2, slots, 128), BF16),
            pltpu.VMEM((16, ma, zd // 2, slots, 128), BF16),
            pltpu.VMEM((kk * slots // 2, 128), F32),
            pltpu.VMEM((M, M), BF16),
            pltpu.VMEM((2 * M, NPHI), BF16),
            pltpu.VMEM((NPHI, 2 * M), BF16),
            pltpu.VMEM((2 * M, NPHI), BF16),
            pltpu.VMEM((NPHI, 2 * M), BF16),
            pltpu.VMEM((zd // 2, NPHI, 256), F32),
            pltpu.VMEM((NPHI, 256), BF16),
            pltpu.VMEM((8, ma, zd // 2, slots, 128), BF16),
            pltpu.VMEM((8, ma, zd // 2, slots, 128), BF16),
            pltpu.VMEM((8, nx, slots // 2, kd, 128), BF16),
            pltpu.VMEM((8, nx, slots // 2, kd, 128), BF16),
            dma((2, slots)), dma((slots,)), dma((2,)),
            dma((16,)), dma((16,)), dma((8,)), dma((8,)),
            dma, dma, dma, dma,
            dma((16,)), dma((16,)), dma((8,)), dma((8, slots // 4)),
        ],
        compiler_params=pltpu.CompilerParams(
            collective_id=1, has_side_effects=True, vmem_limit_bytes=60 * 2**20
        ),
    )(to_rows(forward_coef), to_rows(adjoint_coef), radial_table, jnp.asarray(fourier), jnp.asarray(fourier_t),
      jnp.asarray(cheb), jnp.asarray(cheb_t), radial_count, mode_blocks)
    blocks = rows.reshape(slots, kd * 2, nbs, 2, 128).transpose(0, 1, 3, 2, 4)
    return blocks.reshape(forward_coef.shape)


def solution(mesh):
    placed = (P("ma", "zg", None, None, None), P("ma", "zg", None, None, None), P("ma", None, None), P(), P())
    return jax.shard_map(
        functools.partial(body, MA_DIMS), mesh=mesh, in_specs=placed,
        out_specs=P("ma", "zg", None, None, None), check_vma=False,
    )
```
